768 devices in a mesh: dp: 32 (over y, z_hi, core), mp: 6 (over z_lo), group: 4 (over x).
Axes of the slice: x: 4, y: 8, z: 12 (z_hi: 2, z_lo: 6; z = z_hi * 6 + z_lo), core: 2. Of those that a mesh axis runs over, the one named last changes fastest.
Arguments:
- frames: bfloat16 [55296, 1024], P(('dp', 'mp')), may hold values from -6 to 6
- frame_keep: int32 [55296], P(('dp', 'mp')), may hold values 0 or 1
- destination: int32 [13824, 1], P(('dp', 'mp')), may hold values from 0 to 31; in each aligned block of 72 rows (0 to 71, 72 to 143, ...) at most 3 rows name the same one
- ln_gain: float32 [1024], replicated, may hold values from 0.1 to 1.9
- ln_bias: float32 [1024], replicated, may hold values from -3 to 3
- w_in: bfloat16 [1024, 4096], P(None, 'group'), may hold values from -0.1875 to 0.1875
- w_out: bfloat16 [4096, 1024], P('group'), may hold values from -0.09375 to 0.09375
- upstream: bfloat16 [73728, 1024], P(('dp', 'mp')), may hold values from -6 to 6
Outputs:
- encoded: bfloat16 [73728, 1024], P(('dp', 'mp'))
- w_in_grad: float32 [1024, 4096], P('dp', 'group')
- w_out_grad: float32 [4096, 1024], P('group', 'dp')
The draws below stay inside these ranges and needn't reach their ends.
Inputs may be any that keep to these rules, and one draw needn't show every extreme that they name: At most 3 blocks of one device have the same destination, and in every draw some device sends exactly 3 blocks to one destination.
All inputs are finite; a program needn't handle non-finite values. No bound on the sum of `frame_keep` on one device may be relied on, other than what follows from the above.
Results may differ from the reference program's by a relative error of at most 0.024.
Values may be sent and summed in bfloat16 or wider, within the bound.
A program may use at most 64 MiB of HBM per device.

```python
import math
import jax
import jax.numpy as jnp
import numpy as np
from jax import lax

D = 1024
FF = 4096
CS = 3
BLK = 4
NB = 72
BLOCKS = 13824
TOKENS = 55296
PACKED = 73728
N_DP = 32
N_MP = 6
N_GROUP = 4


def with_ends(values, own_key, least, high):
    longest = values.shape.index(max(values.shape))
    spots = []
    for shift in (0, 1):
        where = [jax.random.randint(jax.random.fold_in(own_key, axis), (), 0, length) for axis, length in enumerate(values.shape)]
        where[longest] = (where[longest] + shift) % values.shape[longest]
        spots.append(tuple(where))
    return values.at[spots[0]].set(least).at[spots[1]].set(high)


def levels(rng, extent, cuts, least, largest):
    def one(position, parts):
        heights = jax.random.uniform(jax.random.fold_in(jax.random.fold_in(rng, 6), position), (parts,), jnp.float32, least / len(cuts), largest / len(cuts))
        return jnp.repeat(jnp.exp(heights), extent[position] // parts).reshape((-1,) + (1,) * (len(extent) - position - 1))

    gain = one(*cuts[0])
    for cut in cuts[1:]:
        gain = gain * one(*cut)
    return gain


def deal_out(own_key, own, number, rows, amount, top, reach, skew):
    ranking = jax.random.permutation(own_key, amount)
    packed, ordinary = shares(amount, rows * top, reach, skew, True), shares(amount, rows * top, reach, skew, False)
    places = jnp.arange(amount)

    def named(sizes, rotation):
        used = int((sizes > 0).sum())
        fixed = max(1, used // 4)
        shifted = fixed + (places - fixed + rotation * (used - fixed)) % max(1, amount - fixed)
        return jnp.zeros((amount,), jnp.int32).at[ranking[jnp.where(places < fixed, places, shifted)]].set(jnp.asarray(sizes, jnp.int32))

    sizes = jnp.where(number % 4 == 0, named(packed, number // 4), named(ordinary, number - number // 4 - 1))
    mixed = jax.random.permutation(jax.random.fold_in(own, 3), amount)
    donor, taker = mixed[0:amount // 2 * 2:2], mixed[1:amount // 2 * 2:2]
    margin = jnp.minimum(sizes[donor] - 1, reach - sizes[taker]) // 2
    margin = jnp.where((donor == ranking[0]) | (taker == ranking[0]) | (sizes[taker] == 0), 0, jnp.maximum(margin, 0))
    shifted = jax.random.randint(jax.random.fold_in(own, 4), (amount // 2,), 0, 1 << 20) % (margin + 1)
    sizes = sizes.at[donor].add(-shifted).at[taker].add(shifted)
    labels = jnp.searchsorted(jnp.cumsum(sizes), jnp.arange(rows * top), side="right").astype(jnp.int32)
    table = labels.reshape(top, rows).T
    table = table[jax.random.permutation(jax.random.fold_in(own, 1), rows)]
    rotation = jax.random.randint(jax.random.fold_in(own, 2), (rows, 1), 0, top)
    return jnp.take_along_axis(table, (jnp.arange(top)[None, :] + rotation) % top, axis=1)


def shares(count, total, bound, slope, full):
    weights = [(1 << 20) // math.isqrt(standing ** slope) + 1 for standing in range(1, count + 1)]
    largest = bound if full else min(bound, max(-(-total // count), total * weights[0] // sum(weights)))
    least = 1 if total - largest >= count - 1 else 0
    holding, surplus = [largest] + [least] * (count - 1), total - largest - least * (count - 1)
    while surplus > 0:
        free = [i for i in range(1, count) if holding[i] < largest] or [i for i in range(1, count) if holding[i] < bound]
        pool, remaining = sum([weights[i] for i in free]), surplus
        for i in free:
            addition = min(bound - holding[i], max(1, remaining * weights[i] // pool), surplus)
            holding[i] = holding[i] + addition
            surplus = surplus - addition
    return np.array(holding)


def gaussian(own_key, extent, spread, bound, split=(), kind=jnp.bfloat16):
    values = spread * jax.random.normal(own_key, extent, jnp.float32)
    if split:
        values = values * levels(own_key, extent, split, -0.22, 0.18)
    return jnp.clip(values, -bound, bound).astype(kind)


def setup_inputs(seed: int = 0) -> dict:
    key_of = jax.random.split(jax.random.key(seed), 9)
    frames = gaussian(key_of[0], (TOKENS, D), 1.0, 6.0, ((0, 192),))
    frame_keep = with_ends((jax.random.randint(key_of[1], (TOKENS,), 0, 4) < 3).astype(jnp.int32), jax.random.fold_in(key_of[1], 1), 0, 1)
    destination_keys = jax.random.split(jax.random.fold_in(key_of[2], 1), BLOCKS // NB)
    destination_turns = jax.random.permutation(jax.random.fold_in(key_of[2], 3), BLOCKS // NB)
    destination = jax.vmap(lambda own, number: deal_out(jax.random.fold_in(key_of[2], 2), own, number, NB, N_DP, 1, CS, 2))(destination_keys, destination_turns).reshape((BLOCKS, 1))
    ln_gain = jnp.clip(1.0 + 0.18 * jax.random.normal(key_of[3], (D,), jnp.float32), 0.1, 1.9)
    ln_bias = gaussian(key_of[4], (D,), 0.5, 3.0, (), jnp.float32)
    w_in = gaussian(key_of[5], (D, FF), D ** -0.5, 0.1875, ((1, 4),))
    w_out = gaussian(key_of[6], (FF, D), FF ** -0.5, 0.09375, ((0, 4),))
    upstream = gaussian(key_of[7], (PACKED, D), 1.0, 6.0, ((0, 192),))
    return dict(frames=frames, frame_keep=frame_keep, destination=destination, ln_gain=ln_gain, ln_bias=ln_bias, w_in=w_in, w_out=w_out, upstream=upstream)


def reference(frames, frame_keep, destination, ln_gain, ln_bias, w_in, w_out, upstream):
    dev_count = N_DP * N_MP
    features = frames.astype(jnp.float32)
    row_mean = lax.optimization_barrier(jnp.mean(features, axis=1, keepdims=True))
    centered = features - row_mean
    row_var = lax.optimization_barrier(jnp.mean(centered * centered, axis=1, keepdims=True))
    normed = (centered * lax.rsqrt(row_var + 1e-05) * ln_gain + ln_bias).astype(jnp.bfloat16)
    preact = jnp.dot(normed, w_in, preferred_element_type=jnp.float32)
    hidden = (preact * jax.nn.sigmoid(preact)).astype(jnp.bfloat16)
    local_ff = FF // N_GROUP
    branch = jnp.zeros((TOKENS, D), jnp.float32)
    for group_pos in range(N_GROUP):
        lower = group_pos * local_ff
        partial_value = jnp.dot(hidden[:, lower:lower + local_ff], w_out[lower:lower + local_ff], preferred_element_type=jnp.float32)
        rounded = lax.optimization_barrier(partial_value.astype(jnp.bfloat16))
        branch = branch + rounded.astype(jnp.float32)
    live_rows = frame_keep.astype(jnp.float32)[:, None]
    result = (live_rows * (features + 0.5 * branch)).astype(jnp.bfloat16)
    target = destination[:, 0].reshape(dev_count, NB)
    chosen = (target[:, :, None] == jnp.arange(N_DP, dtype=jnp.int32)[None, None, :]).astype(jnp.int32)
    before = jnp.cumsum(chosen, axis=1) - chosen
    rank_in = lax.optimization_barrier(jnp.sum(before * chosen, axis=2)).astype(jnp.int32)
    dev_index = jnp.arange(dev_count, dtype=jnp.int32)
    source_dev = dev_index // N_MP
    model_dev = dev_index % N_MP
    receiver = target * N_MP + model_dev[:, None]
    base_row = receiver * (N_DP * CS * BLK) + source_dev[:, None] * (CS * BLK) + rank_in * BLK
    pos = (base_row[:, :, None] + jnp.arange(BLK, dtype=jnp.int32)[None, None, :]).reshape(-1).astype(jnp.int32)
    encoded = jnp.zeros((PACKED, D), jnp.bfloat16).at[pos].set(result)
    gathered = upstream[pos].astype(jnp.float32)
    grad_scale = float(TOKENS) ** (-0.5)
    row_grad = (0.5 * grad_scale * live_rows * gathered).astype(jnp.bfloat16)
    w_out_grad = jnp.dot(hidden.T, row_grad, preferred_element_type=jnp.float32)
    back_hidden = jnp.dot(row_grad, w_out.T, preferred_element_type=jnp.float32)
    sigmoid_pre = jax.nn.sigmoid(preact)
    act_grad = (back_hidden * (sigmoid_pre + preact * sigmoid_pre * (1.0 - sigmoid_pre))).astype(jnp.bfloat16)
    w_in_grad = jnp.dot(normed.T, act_grad, preferred_element_type=jnp.float32)
    return (encoded, w_in_grad, w_out_grad)
```

```python
import functools
import jax
import jax.numpy as jnp
from jax import lax
from jax.experimental import pallas as pl
from jax.experimental.pallas import tpu as pltpu
from jax.sharding import PartitionSpec as P

MESH = pl.DeviceIdType.MESH
NX = 4
NC = 2
NZH = 2
LANE = 128
ROWS16 = 16
F32 = jnp.float32
BF16 = jnp.bfloat16
I32 = jnp.int32


def iota(shape, axis):
    return lax.broadcasted_iota(I32, shape, axis)


def dot(a, b):
    return jnp.dot(a, b, preferred_element_type=F32)


def kernel(
    dims,
    dest_ref,
    keep_ref,
    frames_ref,
    gain_ref,
    bias_ref,
    w_in_hbm,
    w_out_hbm,
    up_ref,
    enc_ref,
    gin_ref,
    gout_ref,
    w_in,
    w_out,
    msg,
    arr,
    tok,
    ups,
    ups_t,
    back,
    nrm_t,
    hid,
    act,
    g_out,
    g_in,
    r_out,
    r_in,
    s_out,
    s_in,
    l_z,
    l_y,
    fin,
    asm,
    swp,
    p_own,
    p_oth,
    p_rcv,
    q_sum,
    q_rcv,
    w_sem,
    a_snd,
    a_rcv,
    u_snd,
    u_rcv,
    t_snd,
    t_rcv,
    o_snd,
    o_rcv,
    i_snd,
    i_rcv,
    z_snd,
    z_rcv,
    y_snd,
    y_rcv,
    f_snd,
    f_rcv,
    c_snd,
    c_rcv,
    p_snd,
    p_rsm,
    q_snd,
    q_rsm,
    e_snd,
    e_rcv,
):
    ny, nzl, cap, run, scale = dims
    nz = NZH * nzl
    rows, width = up_ref.shape
    half = w_in.shape[1]
    slab = rows // ny
    pair_rows = cap * run
    panels = half // LANE
    own_rows = width // (ny * NZH)
    prow = panels * own_rows
    piece = fin.shape[2]
    quarter = rows // NX
    ygroup = ny // NX

    dp = lax.axis_index("dp")
    y = lax.div(dp, 4)
    zh = lax.rem(lax.div(dp, 2), 2)
    c = lax.rem(dp, 2)
    zl = lax.axis_index("mp")
    x = lax.axis_index("group")
    z = zh * nzl + zl
    pc = 1 - c

    def wrap(v, n):
        return lax.rem(v + n, n)

    def at_y(v):
        return {"dp": v * 4 + zh * 2 + c}

    def at_z(v):
        return {"dp": y * 4 + lax.div(v, nzl) * 2 + c, "mp": lax.rem(v, nzl)}

    def at_x(v):
        return {"group": v}

    partner = {"dp": y * 4 + zh * 2 + pc}

    started = []

    def send(src, dst, snd, rcv, where):
        copy = pltpu.make_async_remote_copy(
            src_ref=src, dst_ref=dst, send_sem=snd, recv_sem=rcv, device_id=where, device_id_type=MESH
        )
        copy.start()
        started.append(copy)
        return copy

    get_w_in = pltpu.make_async_copy(w_in_hbm.at[:, pl.ds(pl.multiple_of(c * half, half), half)], w_in, w_sem.at[0])
    get_w_out = pltpu.make_async_copy(w_out_hbm.at[pl.ds(pl.multiple_of(c * half, half), half), :], w_out, w_sem.at[1])
    get_w_out.start()
    get_w_in.start()

    barrier = pltpu.get_barrier_semaphore()
    greeted = 0
    kinds = [(g, dz, dc) for g in range(ygroup) for dz in range(2) for dc in range(2)]

    def a2a_id(yy, dz, dc):
        zz = (1 - zh) if dz else zh
        cc = pc if dc else c
        return {"dp": yy * 4 + zz * 2 + cc}

    sources = []
    for g, dz, dc in kinds:
        if dz or dc:
            sources.append(a2a_id(wrap(y - x - NX * g + ny, ny), dz, dc))
    sources += [at_y(wrap(y - d, ny)) for d in range(1, ny)]
    sources += [at_z(wrap(z - d, nz)) for d in range(1, nz)]
    sources += [at_x(wrap(x - d, NX)) for d in range(1, NX)]
    sources += [partner]
    for where in sources:
        pl.semaphore_signal(barrier, inc=1, device_id=where, device_id_type=MESH)

    nb = dest_ref.shape[1]
    nf = nb * run
    bi, bj = iota((nb, nb), 0), iota((nb, nb), 1)
    drow = jnp.broadcast_to(dest_ref[...], (nb, nb))
    dcol = jnp.sum(jnp.where(bi == bj, drow, 0), axis=1, keepdims=True)
    rank = jnp.sum(jnp.where((dcol == drow) & (bi < bj), 1, 0), axis=0, keepdims=True)
    slot = (dest_ref[...] * cap + rank).astype(F32).astype(BF16)
    spread = (iota((nb, nf), 0) == lax.div(iota((nb, nf), 1), run)).astype(F32).astype(BF16)
    slot_f = dot(jnp.broadcast_to(slot, (8, nb)), spread)[0:1, :]
    nm = len(kinds)
    mi = iota((nm * ROWS16, 1), 0)
    mk, mr = lax.div(mi, ROWS16), lax.rem(mi, ROWS16)
    mg, mdz, mdc = lax.div(mk, 4), lax.rem(lax.div(mk, 2), 2), lax.rem(mk, 2)
    my = lax.rem(y + x + NX * mg, ny)
    mzh = lax.rem(zh + mdz, 2)
    mc = lax.rem(c + mdc, 2)
    want = ((my * 4 + mzh * 2 + mc) * cap + lax.div(mr, run)).astype(F32)
    shape = (nm * ROWS16, nf)
    hit = (
        (jnp.broadcast_to(slot_f, shape) == jnp.broadcast_to(want, shape))
        & (lax.rem(iota(shape, 1), run) == jnp.broadcast_to(lax.rem(mr, run), shape))
        & (jnp.broadcast_to(mr, shape) < pair_rows)
    )
    place = jnp.where(hit, 1.0, 0.0)
    msg[:, :width] = dot(place.astype(BF16), frames_ref[...]).astype(BF16)
    keep_row = keep_ref[...].astype(F32)
    keep_col = jnp.sum(place * keep_row, axis=1, keepdims=True)
    msg[:, width:] = jnp.broadcast_to(keep_col, (nm * ROWS16, LANE)).astype(BF16)
    mine = pl.ds(pl.multiple_of(c * rows, rows), rows)
    theirs = pl.ds(pl.multiple_of(pc * rows, rows), rows)
    ups[mine, :] = (scale * up_ref[...].astype(F32)).astype(BF16)

    pl.semaphore_wait(barrier, len(sources))

    a2a = []
    for k, (g, dz, dc) in enumerate(kinds):
        spot = pl.ds(pl.multiple_of((g * 4 + zh * 2 + c) * ROWS16, ROWS16), ROWS16)
        part = msg.at[pl.ds(k * ROWS16, ROWS16), :]
        copy = pltpu.make_async_remote_copy(
            src_ref=part,
            dst_ref=arr.at[spot, :],
            send_sem=a_snd.at[k],
            recv_sem=a_rcv.at[k],
            device_id=a2a_id(lax.rem(y + x + NX * g, ny), dz, dc),
            device_id_type=MESH,
        )
        if k == 0:
            local = pltpu.make_async_copy(part, arr.at[spot, :], a_rcv.at[k])

            @pl.when(x == 0)
            def _(local=local):
                local.start()

            @pl.when(x != 0)
            def _(copy=copy):
                copy.start()
        else:
            copy.start()
        a2a.append(copy)
    ucopy = send(ups.at[mine, :], ups.at[mine, :], u_snd.at[0], u_rcv.at[0], partner)

    get_w_out.wait()
    for where in (mine, theirs):
        if where is theirs:
            ucopy.wait_recv()
        u = ups[where, :]
        back[where, :] = lax.dot_general(u, w_out[...], (((1,), (1,)), ((), ())), preferred_element_type=F32)
        ups_t[:, where] = u.T
    get_w_in.wait()

    for k in range(nm):
        if k == 0:

            @pl.when(x == 0)
            def _():
                local.wait()

            @pl.when(x != 0)
            def _():
                a2a[0].wait()
        else:
            a2a[k].wait()

    cq = ygroup * slab
    ci, cj = iota((cq, nm * ROWS16), 0), iota((cq, nm * ROWS16), 1)
    squeeze = (cj == lax.div(ci, pair_rows) * ROWS16 + lax.rem(ci, pair_rows)).astype(F32).astype(BF16)
    compact = dot(squeeze, arr[...]).astype(BF16)

    def rows_of(origin, g):
        ys = lax.rem(y - origin - NX * g + 2 * ny, ny)
        return tok.at[pl.ds(pl.multiple_of(c * rows + ys * slab, ROWS16), slab), :]

    def t_at(second, o, g):
        return second * 8 + o * 2 + g

    xn, xp, xo = wrap(x + 1, NX), wrap(x - 1, NX), wrap(x + 2, NX)
    origins = {0: x, 1: xn, 2: xo, 3: xp}

    def t_send(o, g, second, slot_at_receiver, tag, where):
        ref = rows_of(origins[o], g)
        return send(ref, ref, t_snd.at[tag], t_rcv.at[t_at(second, slot_at_receiver, g)], where)

    waits = {}
    for g in range(ygroup):
        rows_of(x, g)[...] = compact[g * slab : (g + 1) * slab, :]
        waits[3, g] = t_send(0, g, 0, 3, g, at_x(xn))
        waits[1, g] = t_send(0, g, 0, 1, 2 + g, at_x(xp))
        waits["c", 0, g] = t_send(0, g, 1, 0, 4 + g, partner)
    waits[3, 0].wait_recv()
    waits[2, 0] = t_send(3, 0, 0, 2, 6, at_x(xn))
    waits["c", 3, 0] = t_send(3, 0, 1, 3, 8, partner)
    waits[1, 1].wait_recv()
    waits[2, 1] = t_send(1, 1, 0, 2, 7, at_x(xp))
    waits["c", 1, 1] = t_send(1, 1, 1, 1, 9, partner)
    waits[3, 1].wait_recv()
    waits["c", 3, 1] = t_send(3, 1, 1, 3, 10, partner)
    waits[1, 0].wait_recv()
    waits["c", 1, 0] = t_send(1, 0, 1, 1, 11, partner)
    for g in range(ygroup):
        waits[2, g].wait_recv()
        waits["c", 2, g] = t_send(2, g, 1, 2, 12 + g, partner)
    for o in range(NX):
        for g in range(ygroup):
            waits["c", o, g].wait_recv()

    step_rows = LANE
    for t in range(2 * rows // step_rows):
        at = pl.ds(t * step_rows, step_rows)
        feat = tok[at, :width].astype(F32)
        live = tok[at, width:][:, 0:1].astype(F32)
        mean = jnp.mean(feat, axis=1, keepdims=True)
        cen = feat - mean
        var = jnp.mean(cen * cen, axis=1, keepdims=True)
        norm = (cen * lax.rsqrt(var + 1e-05) * gain_ref[...] + bias_ref[...]).astype(BF16)
        nrm_t[:, at] = norm.T
        pre = dot(norm, w_in[...])
        sig = jax.nn.sigmoid(pre)
        hid[at, :] = (live * (pre * sig)).astype(BF16)
        act[at, :] = (live * back[at, :] * (sig + pre * sig * (1.0 - sig))).astype(BF16)

    def gradient(left, right, out):
        block = 2 * LANE
        for b in range(width // block):
            val = dot(left[pl.ds(b * block, block), :], right[...]).astype(BF16)
            for u in range(block // own_rows):
                unit = b * (block // own_rows) + u
                for p in range(panels):
                    out[unit % NZH, unit // NZH, pl.ds(p * own_rows, own_rows), :] = val[
                        u * own_rows : (u + 1) * own_rows, p * LANE : (p + 1) * LANE
                    ]

    def start_of(j):
        return pl.multiple_of(jnp.minimum(j * piece, prow - piece), ROWS16)

    ysteps = ny // 2
    ochain = {}

    def o_step(s):
        for d in range(2):
            sign = 1 - 2 * d
            for h in range(2):
                first = 1 if d == h else 2
                if s < first:
                    continue
                target = wrap(y + sign * (ysteps + 1 - s), ny)
                if s == first:
                    src = g_out.at[h, target]
                else:
                    ochain[d, h, s - 1].wait_recv()
                    src = r_out.at[d, h, s - 2]
                    src[...] = (src[...].astype(F32) + g_out[h, target].astype(F32)).astype(BF16)
                tag = (d * 2 + h) * ysteps + s - 1
                ochain[d, h, s] = send(
                    src, r_out.at[d, h, s - 1], o_snd.at[tag], o_rcv.at[tag], at_y(wrap(y + sign, ny))
                )

    zsteps = nz // 2
    ichain = {}
    hy = ny // 2

    def i_own(h, v):
        return g_in.at[lax.div(v, nzl), pl.ds(h * hy, hy), pl.ds(start_of(lax.rem(v, nzl)), piece), :]

    def i_step(s):
        for d in range(2):
            sign = 1 - 2 * d
            for h in range(2):
                first = 1 if d == h else 2
                if s < first:
                    continue
                own = i_own(h, wrap(z + sign * (zsteps + 1 - s), nz))
                if s == first:
                    src = own
                else:
                    ichain[d, h, s - 1].wait_recv()
                    src = r_in.at[d, h, s - 2]
                    src[...] = (src[...].astype(F32) + own[...].astype(F32)).astype(BF16)
                tag = (d * 2 + h) * zsteps + s - 1
                ichain[d, h, s] = send(
                    src, r_in.at[d, h, s - 1], i_snd.at[tag], i_rcv.at[tag], at_z(wrap(z + sign, nz))
                )

    gradient(ups_t, hid, g_out)
    o_step(1)
    gradient(nrm_t, act, g_in)
    i_step(1)
    p_oth[...] = dot(hid[theirs, :], w_out[...]).astype(BF16)
    pcopy = send(p_oth, p_rcv, p_snd.at[0], p_rsm.at[0], partner)
    o_step(2)
    i_step(2)
    p_own[...] = dot(hid[mine, :], w_out[...])
    o_step(3)
    pcopy.wait_recv()
    q_sum[...] = (p_own[...] + p_rcv[...].astype(F32)).astype(BF16)
    qcopies = []
    for d in range(1, NX):
        to = wrap(x + d, NX)
        part = q_sum.at[pl.ds(pl.multiple_of(to * quarter, quarter), quarter), :]
        qcopies.append(send(part, q_rcv.at[d - 1], q_snd.at[d - 1], q_rsm.at[d - 1], at_x(to)))
    i_step(3)
    o_step(4)
    i_step(4)

    zcopies = []
    for h in range(2):
        ochain[0, h, ysteps].wait_recv()
        ochain[1, h, ysteps].wait_recv()
        s_out[h] = (
            g_out[h, y].astype(F32)
            + r_out[0, h, ysteps - 1].astype(F32)
            + r_out[1, h, ysteps - 1].astype(F32)
        ).astype(BF16)
    for d in range(1, nz):
        to = wrap(z + d, nz)
        part = s_out.at[lax.div(to, nzl), pl.ds(start_of(lax.rem(to, nzl)), piece), :]
        zcopies.append(send(part, l_z.at[d - 1], z_snd.at[d - 1], z_rcv.at[d - 1], at_z(to)))
    i_step(5)

    for q in qcopies:
        q.wait_recv()
    xrows = pl.ds(pl.multiple_of(x * quarter, quarter), quarter)
    total = q_sum[xrows, :].astype(F32)
    for d in range(1, NX):
        total = total + q_rcv[d - 1].astype(F32)
    trows = pl.ds(pl.multiple_of(c * rows + x * quarter, ROWS16), quarter)
    feat = tok[trows, :width].astype(F32)
    live = tok[trows, width:][:, 0:1].astype(F32)
    enc_ref[xrows, :] = (live * (feat + 0.5 * total)).astype(BF16)
    ecopies = []
    for d in range(1, NX):
        part = enc_ref.at[xrows, :]
        ecopies.append(send(part, part, e_snd.at[d - 1], e_rcv.at[d - 1], at_x(wrap(x + d, NX))))
    i_step(6)

    for h in range(2):
        ichain[0, h, zsteps].wait_recv()
        ichain[1, h, zsteps].wait_recv()
        s_in[pl.ds(h * hy, hy)] = (
            i_own(h, z)[...].astype(F32)
            + r_in[0, h, zsteps - 1].astype(F32)
            + r_in[1, h, zsteps - 1].astype(F32)
        ).astype(BF16)
    ycopies = []
    for d in range(1, ny):
        to = wrap(y + d, ny)
        ycopies.append(send(s_in.at[to], l_y.at[d - 1], y_snd.at[d - 1], y_rcv.at[d - 1], at_y(to)))

    for q in zcopies:
        q.wait_recv()
    sum_out = s_out[zh, pl.ds(start_of(zl), piece), :].astype(F32)
    for d in range(1, nz):
        sum_out = sum_out + l_z[d - 1].astype(F32)
    fin[1, zl] = sum_out.astype(BF16)
    for q in ycopies:
        q.wait_recv()
    sum_in = s_in[y].astype(F32)
    for d in range(1, ny):
        sum_in = sum_in + l_y[d - 1].astype(F32)
    fin[0, zl] = sum_in.astype(BF16)

    fcopies = []
    for d in range(1, nzl):
        to = wrap(zl + d, nzl)
        part = fin.at[:, zl]
        fcopies.append(send(part, part, f_snd.at[d - 1], f_rcv.at[d - 1], {"dp": dp, "mp": to}))
    for q in fcopies:
        q.wait_recv()
    for u in range(prow // ROWS16):
        row = u * ROWS16
        j = next(j for j in range(nzl) if min(j * piece, prow - piece) <= row < min(j * piece, prow - piece) + piece)
        off = row - min(j * piece, prow - piece)
        for t in range(2):
            asm[t, row // own_rows, pl.ds(row % own_rows, ROWS16), :] = fin[t, j, pl.ds(off, ROWS16), :]
    core_rows = own_rows // NC
    ccopy = send(
        asm.at[:, :, pl.ds(pl.multiple_of(pc * core_rows, core_rows), core_rows), :],
        swp,
        c_snd.at[0],
        c_rcv.at[0],
        partner,
    )
    ccopy.wait_recv()
    for t, ref in enumerate((gin_ref, gout_ref)):
        for p in range(panels):
            own = asm[t, p, pl.ds(pl.multiple_of(c * core_rows, core_rows), core_rows), :].astype(F32)
            other = swp[t, p].astype(F32)
            ref[:, pl.ds(pl.multiple_of(c * half + p * LANE, LANE), LANE)] = own
            ref[:, pl.ds(pl.multiple_of(pc * half + p * LANE, LANE), LANE)] = other

    for q in ecopies:
        q.wait_recv()
    for q in started:
        q.wait_send()


def shards(ny, nzl, frames, frame_keep, destination, ln_gain, ln_bias, w_in, w_out, upstream):
    nf, width = frames.shape
    nb = destination.shape[0]
    run = nf // nb
    rows = upstream.shape[0]
    cap = rows // (run * ny * 4)
    units = w_in.shape[1]
    half = units // NC
    own_rows = width // (ny * NZH)
    panels = half // LANE
    prow = panels * own_rows
    piece = -(-prow // (nzl * ROWS16)) * ROWS16
    nz = NZH * nzl
    ygroup = ny // NX
    nm = ygroup * 4
    grad_scale = float(nf * ny * 4 * nzl) ** (-0.5)
    quarter = rows // NX
    ysteps, zsteps = ny // 2, nz // 2
    core_rows = own_rows // NC
    dma = pltpu.SemaphoreType.DMA
    vm = pltpu.VMEM
    pairs = [2, nm, 1, 16, 4 * ysteps, 4 * zsteps, nz - 1, ny - 1, nzl - 1, 1, 1, NX - 1, NX - 1]
    sems = []
    for i, n in enumerate(pairs):
        sems += [dma((n,))] if i == 0 else [dma((n,)), dma((n,))]
    vspec = pl.BlockSpec(memory_space=pltpu.VMEM)
    aspec = pl.BlockSpec(memory_space=pl.ANY)
    enc, gin, gout = pl.pallas_call(
        functools.partial(kernel, (ny, nzl, cap, run, 0.5 * grad_scale)),
        out_shape=(
            jax.ShapeDtypeStruct((rows, width), BF16),
            jax.ShapeDtypeStruct((core_rows, units), F32),
            jax.ShapeDtypeStruct((core_rows, units), F32),
        ),
        in_specs=[vspec, vspec, vspec, vspec, vspec, aspec, aspec, vspec],
        out_specs=(vspec, vspec, vspec),
        scratch_shapes=[
            vm((width, half), BF16),
            vm((half, width), BF16),
            vm((nm * ROWS16, width + LANE), BF16),
            vm((nm * ROWS16, width + LANE), BF16),
            vm((NC * rows, width + LANE), BF16),
            vm((NC * rows, width), BF16),
            vm((width, NC * rows), BF16),
            vm((NC * rows, half), F32),
            vm((width, NC * rows), BF16),
            vm((NC * rows, half), BF16),
            vm((NC * rows, half), BF16),
            vm((NZH, ny, prow, LANE), BF16),
            vm((NZH, ny, prow, LANE), BF16),
            vm((2, 2, ysteps, prow, LANE), BF16),
            vm((2, 2, zsteps, ny // 2, piece, LANE), BF16),
            vm((NZH, prow, LANE), BF16),
            vm((ny, piece, LANE), BF16),
            vm((nz - 1, piece, LANE), BF16),
            vm((ny - 1, piece, LANE), BF16),
            vm((2, nzl, piece, LANE), BF16),
            vm((2, panels, own_rows, LANE), BF16),
            vm((2, panels, core_rows, LANE), BF16),
            vm((rows, width), F32),
            vm((rows, width), BF16),
            vm((rows, width), BF16),
            vm((rows, width), BF16),
            vm((NX - 1, quarter, width), BF16),
        ]
        + sems,
        compiler_params=pltpu.CompilerParams(
            collective_id=0, has_side_effects=True, vmem_limit_bytes=56 * 1024 * 1024
        ),
        name="ffn_step",
    )(
        destination.reshape(1, nb),
        frame_keep.reshape(1, nf),
        frames,
        ln_gain.reshape(1, width),
        ln_bias.reshape(1, width),
        w_in,
        w_out,
        upstream,
    )
    return (enc, gin, gout.T)


def solution(mesh):
    placed = (
        P(("dp", "mp"), None),
        P(("dp", "mp")),
        P(("dp", "mp"), None),
        P(),
        P(),
        P(None, "group"),
        P("group", None),
        P(("dp", "mp"), None),
    )
    ny = mesh.shape["dp"] // (NZH * NC)
    return jax.shard_map(
        functools.partial(shards, ny, mesh.shape["mp"]),
        mesh=mesh,
        in_specs=placed,
        out_specs=(P(("dp", "mp"), None), P("dp", "group"), P("group", "dp")),
        check_vma=False,
    )
```

```python
import functools
import jax
import jax.numpy as jnp
from jax import lax
from jax.experimental import pallas as pl
from jax.experimental.pallas import tpu as pltpu
from jax.sharding import PartitionSpec as P

MESH = pl.DeviceIdType.MESH
NX = 4
NC = 2
NZH = 2
LANE = 128
ROWS16 = 16
F32 = jnp.float32
BF16 = jnp.bfloat16
I32 = jnp.int32
OPARTS = 2
IPARTS = 2


def iota(shape, axis):
    return lax.broadcasted_iota(I32, shape, axis)


def dot(a, b):
    return jnp.dot(a, b, preferred_element_type=F32)


def kernel(
    dims,
    dest_ref,
    keep_ref,
    frames_ref,
    gain_ref,
    bias_ref,
    w_in_hbm,
    w_out_hbm,
    up_ref,
    enc_ref,
    gin_ref,
    gout_ref,
    w_in,
    w_out,
    msg,
    arr,
    tok,
    ups,
    ups_t,
    back,
    nrm_t,
    hid,
    act,
    g_out,
    g_in,
    r_out,
    r_in,
    s_out,
    s_in,
    l_z,
    l_y,
    pce,
    fin,
    p_own,
    p_oth,
    p_rcv,
    q_sum,
    q_rcv,
    w_sem,
    a_snd,
    a_rcv,
    u_snd,
    u_rcv,
    t_snd,
    t_rcv,
    o_snd,
    o_rcv,
    i_snd,
    i_rcv,
    z_snd,
    z_rcv,
    y_snd,
    y_rcv,
    f_snd,
    f_rcv,
    p_snd,
    p_rsm,
    q_snd,
    q_rsm,
    e_snd,
    e_rcv,
):
    ny, nzl, cap, run, scale = dims
    nz = NZH * nzl
    rows, width = up_ref.shape
    half = w_in.shape[1]
    slab = rows // ny
    pair_rows = cap * run
    panels = half // LANE
    own_rows = width // (ny * NZH)
    prow = panels * own_rows
    core_rows = own_rows // NC
    core_span = panels * core_rows
    per_core = nzl // NC
    piece = pce.shape[1]
    quarter = rows // NX
    ygroup = ny // NX

    dp = lax.axis_index("dp")
    y = lax.div(dp, 4)
    zh = lax.rem(lax.div(dp, 2), 2)
    c = lax.rem(dp, 2)
    zl = lax.axis_index("mp")
    x = lax.axis_index("group")
    z = zh * nzl + zl
    pc = 1 - c

    def wrap(v, n):
        return lax.rem(v + n, n)

    def at_y(v):
        return {"dp": v * 4 + zh * 2 + c}

    def at_z(v):
        return {"dp": y * 4 + lax.div(v, nzl) * 2 + c, "mp": lax.rem(v, nzl)}

    def at_x(v):
        return {"group": v}

    partner = {"dp": y * 4 + zh * 2 + pc}

    started = []

    def send(src, dst, snd, rcv, where):
        copy = pltpu.make_async_remote_copy(
            src_ref=src, dst_ref=dst, send_sem=snd, recv_sem=rcv, device_id=where, device_id_type=MESH
        )
        copy.start()
        started.append(copy)
        return copy

    get_w_in = pltpu.make_async_copy(w_in_hbm.at[:, pl.ds(pl.multiple_of(c * half, half), half)], w_in, w_sem.at[0])
    get_w_out = pltpu.make_async_copy(w_out_hbm.at[pl.ds(pl.multiple_of(c * half, half), half), :], w_out, w_sem.at[1])
    get_w_out.start()
    get_w_in.start()

    barrier = pltpu.get_barrier_semaphore()
    greeted = 0
    kinds = [(g, dz, dc) for g in range(ygroup) for dz in range(2) for dc in range(2)]

    def a2a_id(yy, dz, dc):
        zz = (1 - zh) if dz else zh
        cc = pc if dc else c
        return {"dp": yy * 4 + zz * 2 + cc}

    sources = []
    for g, dz, dc in kinds:
        if dz or dc:
            sources.append(a2a_id(wrap(y - x - NX * g + ny, ny), dz, dc))
    sources += [at_y(wrap(y - d, ny)) for d in range(1, ny)]
    sources += [at_z(wrap(z - d, nz)) for d in range(1, nz)]
    sources += [at_x(wrap(x - d, NX)) for d in range(1, NX)]
    sources += [{"dp": y * 4 + zh * 2 + pc, "mp": wrap(zl - d, nzl)} for d in range(1, nzl)]
    sources += [partner]
    for where in sources:
        pl.semaphore_signal(barrier, inc=1, device_id=where, device_id_type=MESH)

    nb = dest_ref.shape[1]
    nf = nb * run
    bi, bj = iota((nb, nb), 0), iota((nb, nb), 1)
    drow = jnp.broadcast_to(dest_ref[...], (nb, nb))
    dcol = jnp.sum(jnp.where(bi == bj, drow, 0), axis=1, keepdims=True)
    rank = jnp.sum(jnp.where((dcol == drow) & (bi < bj), 1, 0), axis=0, keepdims=True)
    slot = (dest_ref[...] * cap + rank).astype(F32).astype(BF16)
    spread = (iota((nb, nf), 0) == lax.div(iota((nb, nf), 1), run)).astype(F32).astype(BF16)
    slot_f = dot(jnp.broadcast_to(slot, (8, nb)), spread)[0:1, :]
    nm = len(kinds)
    mi = iota((nm * ROWS16, 1), 0)
    mk, mr = lax.div(mi, ROWS16), lax.rem(mi, ROWS16)
    mg, mdz, mdc = lax.div(mk, 4), lax.rem(lax.div(mk, 2), 2), lax.rem(mk, 2)
    my = lax.rem(y + x + NX * mg, ny)
    mzh = lax.rem(zh + mdz, 2)
    mc = lax.rem(c + mdc, 2)
    want = ((my * 4 + mzh * 2 + mc) * cap + lax.div(mr, run)).astype(F32)
    shape = (nm * ROWS16, nf)
    hit = (
        (jnp.broadcast_to(slot_f, shape) == jnp.broadcast_to(want, shape))
        & (lax.rem(iota(shape, 1), run) == jnp.broadcast_to(lax.rem(mr, run), shape))
        & (jnp.broadcast_to(mr, shape) < pair_rows)
    )
    place = jnp.where(hit, 1.0, 0.0)
    msg[:, :width] = dot(place.astype(BF16), frames_ref[...]).astype(BF16)
    keep_row = keep_ref[...].reshape(1, nf).astype(F32)
    keep_col = jnp.sum(place * keep_row, axis=1, keepdims=True)
    msg[:, width:] = jnp.broadcast_to(keep_col, (nm * ROWS16, LANE)).astype(BF16)
    mine = pl.ds(pl.multiple_of(c * rows, rows), rows)
    theirs = pl.ds(pl.multiple_of(pc * rows, rows), rows)

    pl.semaphore_wait(barrier, len(sources))

    a2a = []

    def a2a_send(k):
        g, dz, dc = kinds[k]
        spot = pl.ds(pl.multiple_of((g * 4 + zh * 2 + c) * ROWS16, ROWS16), ROWS16)
        part = msg.at[pl.ds(k * ROWS16, ROWS16), :]
        copy = pltpu.make_async_remote_copy(
            src_ref=part,
            dst_ref=arr.at[spot, :],
            send_sem=a_snd.at[k],
            recv_sem=a_rcv.at[k],
            device_id=a2a_id(lax.rem(y + x + NX * g, ny), dz, dc),
            device_id_type=MESH,
        )
        a2a.append(copy)
        if k:
            copy.start()
            return None
        local = pltpu.make_async_copy(part, arr.at[spot, :], a_rcv.at[k])

        @pl.when(x == 0)
        def _():
            local.start()

        @pl.when(x != 0)
        def _():
            copy.start()

        return local

    def back_of(where):
        u = ups[where, :]
        back[where, :] = lax.dot_general(u, w_out[...], (((1,), (1,)), ((), ())), preferred_element_type=F32)
        ups_t[:, where] = u.T

    locals_of = {}
    for k in range(4):
        locals_of[k] = a2a_send(k)
    local = locals_of[0]
    ups[mine, :] = (scale * up_ref[...].astype(F32)).astype(BF16)
    ucopy = send(ups.at[mine, :], ups.at[mine, :], u_snd.at[0], u_rcv.at[0], partner)
    get_w_out.wait()
    back_of(mine)
    for k in range(4):
        if k:
            a2a[k].wait_send()
        else:

            @pl.when(x != 0)
            def _():
                a2a[0].wait_send()

    for k in range(4, nm):
        a2a_send(k)
    ucopy.wait_recv()
    back_of(theirs)
    get_w_in.wait()

    ci, cj = iota((slab, 4 * ROWS16), 0), iota((slab, 4 * ROWS16), 1)
    squeeze = (cj == lax.div(ci, pair_rows) * ROWS16 + lax.rem(ci, pair_rows)).astype(F32).astype(BF16)

    def rows_of(origin, g):
        ys = lax.rem(y - origin - NX * g + 2 * ny, ny)
        return tok.at[pl.ds(pl.multiple_of(c * rows + ys * slab, ROWS16), slab), :]

    def t_at(second, o, g):
        return second * 8 + o * 2 + g

    xn, xp, xo = wrap(x + 1, NX), wrap(x - 1, NX), wrap(x + 2, NX)
    origins = {0: x, 1: xn, 2: xo, 3: xp}

    def t_send(o, g, second, slot_at_receiver, tag, where):
        ref = rows_of(origins[o], g)
        return send(ref, ref, t_snd.at[tag], t_rcv.at[t_at(second, slot_at_receiver, g)], where)

    waits = {}
    for g in range(ygroup):
        for k in range(g * 4, g * 4 + 4):
            if k == 0:

                @pl.when(x == 0)
                def _():
                    local.wait()

                @pl.when(x != 0)
                def _():
                    a2a[0].wait_recv()
            elif k < 4:
                a2a[k].wait_recv()
            else:
                a2a[k].wait()
        rows_of(x, g)[...] = dot(squeeze, arr[pl.ds(g * 4 * ROWS16, 4 * ROWS16), :]).astype(BF16)
        if g == 0:
            waits[3, g] = t_send(0, g, 0, 3, g, at_x(xn))
            waits[1, g] = t_send(0, g, 0, 1, 2 + g, at_x(xp))
        else:
            waits[1, g] = t_send(0, g, 0, 1, 2 + g, at_x(xp))
            waits[3, g] = t_send(0, g, 0, 3, g, at_x(xn))
        waits["c", 0, g] = t_send(0, g, 1, 0, 4 + g, partner)
    waits[3, 0].wait_recv()
    waits[2, 0] = t_send(3, 0, 0, 2, 6, at_x(xn))
    waits["c", 3, 0] = t_send(3, 0, 1, 3, 8, partner)
    waits[1, 1].wait_recv()
    waits[2, 1] = t_send(1, 1, 0, 2, 7, at_x(xp))
    waits["c", 1, 1] = t_send(1, 1, 1, 1, 9, partner)
    waits[1, 0].wait_recv()
    waits["c", 1, 0] = t_send(1, 0, 1, 1, 11, partner)
    waits[3, 1].wait_recv()
    waits["c", 3, 1] = t_send(3, 1, 1, 3, 10, partner)
    for g in range(ygroup):
        waits[2, g].wait_recv()
        waits["c", 2, g] = t_send(2, g, 1, 2, 12 + g, partner)
    for o in (0, 3, 1, 2):
        for g in range(ygroup):
            waits["c", o, g].wait_recv()

    step_rows = LANE
    for t in range(2 * rows // step_rows):
        at = pl.ds(t * step_rows, step_rows)
        feat = tok[at, :width].astype(F32)
        live = tok[at, width:][:, 0:1].astype(F32)
        mean = jnp.mean(feat, axis=1, keepdims=True)
        cen = feat - mean
        var = jnp.mean(cen * cen, axis=1, keepdims=True)
        norm = (cen * lax.rsqrt(var + 1e-05) * gain_ref[...] + bias_ref[...]).astype(BF16)
        nrm_t[:, at] = norm.T
        pre = dot(norm, w_in[...])
        sig = jax.nn.sigmoid(pre)
        hid[at, :] = (live * (pre * sig)).astype(BF16)
        act[at, :] = (live * back[at, :] * (sig + pre * sig * (1.0 - sig))).astype(BF16)

    def gradient(left, right, out):
        block = 2 * LANE
        for b in range(width // block):
            val = dot(left[pl.ds(b * block, block), :], right[...]).astype(BF16)
            for u in range(block // own_rows):
                unit = b * (block // own_rows) + u
                for e in range(NC):
                    for p in range(panels):
                        row = u * own_rows + e * core_rows
                        out[unit % NZH, unit // NZH, pl.ds((e * panels + p) * core_rows, core_rows), :] = val[
                            row : row + core_rows, p * LANE : (p + 1) * LANE
                        ]

    def start_of(j):
        core_at = lax.div(j, per_core)
        inside = jnp.minimum(lax.rem(j, per_core) * piece, core_span - piece)
        return pl.multiple_of(core_at * core_span + inside, ROWS16)

    ysteps = ny // 2
    ochain = {}
    ocut = OPARTS // NZH
    orows = prow // ocut

    def o_own(q, v):
        return g_out.at[q // ocut, v, pl.ds(q % ocut * orows, orows), :]

    def o_step(phase, s):
        for d in range(2):
            sign = 1 - 2 * d
            for q in range(OPARTS):
                if (d == q % 2) != (phase == 0):
                    continue
                first = 1 + phase
                own = o_own(q, wrap(y + sign * (ysteps + 1 - s), ny))
                if s == first:
                    src = own
                else:
                    ochain[d, q, s - 1].wait_recv()
                    src = r_out.at[d, q, s - 2]
                    src[...] = (src[...].astype(F32) + own[...].astype(F32)).astype(BF16)
                tag = (d * OPARTS + q) * ysteps + s - 1
                ochain[d, q, s] = send(
                    src, r_out.at[d, q, s - 1], o_snd.at[tag], o_rcv.at[tag], at_y(wrap(y + sign, ny))
                )

    zsteps = nz // 2
    ichain = {}
    hy = ny // IPARTS

    def i_own(q, v):
        return g_in.at[lax.div(v, nzl), pl.ds(q * hy, hy), pl.ds(start_of(lax.rem(v, nzl)), piece), :]

    def i_step(phase, s):
        for d in range(2):
            sign = 1 - 2 * d
            for q in range(IPARTS):
                if (d == q % 2) != (phase == 0):
                    continue
                first = 1 + phase
                own = i_own(q, wrap(z + sign * (zsteps + 1 - s), nz))
                if s == first:
                    src = own
                else:
                    ichain[d, q, s - 1].wait_recv()
                    src = r_in.at[d, q, s - 2]
                    src[...] = (src[...].astype(F32) + own[...].astype(F32)).astype(BF16)
                tag = (d * IPARTS + q) * zsteps + s - 1
                ichain[d, q, s] = send(
                    src, r_in.at[d, q, s - 1], i_snd.at[tag], i_rcv.at[tag], at_z(wrap(z + sign, nz))
                )

    gradient(nrm_t, act, g_in)
    i_step(0, 1)
    gradient(ups_t, hid, g_out)
    o_step(0, 1)
    i_step(1, 2)
    p_oth[...] = dot(hid[theirs, :], w_out[...]).astype(BF16)
    o_step(1, 2)
    pcopy = send(p_oth, p_rcv, p_snd.at[0], p_rsm.at[0], partner)
    i_step(0, 2)
    o_step(0, 2)
    p_own[...] = dot(hid[mine, :], w_out[...])
    i_step(1, 3)
    o_step(1, 3)
    i_step(0, 3)
    o_step(0, 3)
    i_step(1, 4)
    o_step(1, 4)
    pcopy.wait_recv()
    q_sum[...] = (p_own[...] + p_rcv[...].astype(F32)).astype(BF16)
    qcopies = []
    for d in range(1, NX):
        to = wrap(x + d, NX)
        part = q_sum.at[pl.ds(pl.multiple_of(to * quarter, quarter), quarter), :]
        qcopies.append(send(part, q_rcv.at[d - 1], q_snd.at[d - 1], q_rsm.at[d - 1], at_x(to)))
    i_step(0, 4)
    o_step(0, 4)
    i_step(1, 5)
    i_step(0, 5)

    zcopies = []
    for q in range(OPARTS):
        ochain[0, q, ysteps].wait_recv()
        ochain[1, q, ysteps].wait_recv()
        s_out[q // ocut, pl.ds(q % ocut * orows, orows), :] = (
            o_own(q, y)[...].astype(F32)
            + r_out[0, q, ysteps - 1].astype(F32)
            + r_out[1, q, ysteps - 1].astype(F32)
        ).astype(BF16)
    for d in range(1, nz):
        to = wrap(z + d, nz)
        part = s_out.at[lax.div(to, nzl), pl.ds(start_of(lax.rem(to, nzl)), piece), :]
        zcopies.append(send(part, l_z.at[d - 1], z_snd.at[d - 1], z_rcv.at[d - 1], at_z(to)))
    i_step(1, 6)
    i_step(0, 6)

    for q in range(IPARTS):
        ichain[0, q, zsteps].wait_recv()
        ichain[1, q, zsteps].wait_recv()
        s_in[pl.ds(q * hy, hy)] = (
            i_own(q, z)[...].astype(F32)
            + r_in[0, q, zsteps - 1].astype(F32)
            + r_in[1, q, zsteps - 1].astype(F32)
        ).astype(BF16)
    ycopies = []
    for d in range(1, ny):
        to = wrap(y + d, ny)
        ycopies.append(send(s_in.at[to], l_y.at[d - 1], y_snd.at[d - 1], y_rcv.at[d - 1], at_y(to)))

    home = lax.div(zl, per_core)
    spot = c * per_core + lax.rem(zl, per_core)

    def gather(t):
        def base(d):
            return pltpu.make_async_remote_copy(
                src_ref=pce.at[t],
                dst_ref=fin.at[t, spot],
                send_sem=f_snd.at[t, d],
                recv_sem=f_rcv.at[t, spot],
                device_id={"dp": y * 4 + zh * 2 + home, "mp": wrap(zl + d, nzl)},
                device_id_type=MESH,
            )

        @pl.when(home == c)
        def _():
            pltpu.make_async_copy(pce.at[t], fin.at[t, spot], f_rcv.at[t, spot]).start()

        @pl.when(home != c)
        def _():
            base(0).start()

        for d in range(1, nzl):
            copy = base(d)
            copy.start()
            started.append(copy)
        return base(0)

    def gathered(t):
        for slot in range(NC * per_core):
            pltpu.make_async_copy(pce.at[t], fin.at[t, slot], f_rcv.at[t, slot]).wait()

    for q in zcopies:
        q.wait_recv()
    sum_out = s_out[zh, pl.ds(start_of(zl), piece), :].astype(F32)
    for d in range(1, nz):
        sum_out = sum_out + l_z[d - 1].astype(F32)
    pce[1] = sum_out.astype(BF16)
    own_out = gather(1)
    for q in qcopies:
        q.wait_recv()
    xrows = pl.ds(pl.multiple_of(x * quarter, quarter), quarter)
    total = q_sum[xrows, :].astype(F32)
    for d in range(1, NX):
        total = total + q_rcv[d - 1].astype(F32)
    trows = pl.ds(pl.multiple_of(c * rows + x * quarter, ROWS16), quarter)
    feat = tok[trows, :width].astype(F32)
    live = tok[trows, width:][:, 0:1].astype(F32)
    enc_ref[xrows, :] = (live * (feat + 0.5 * total)).astype(BF16)
    ecopies = []
    for d in range(1, NX):
        part = enc_ref.at[xrows, :]
        ecopies.append(send(part, part, e_snd.at[d - 1], e_rcv.at[d - 1], at_x(wrap(x + d, NX))))

    for q in ycopies:
        q.wait_recv()
    sum_in = s_in[y].astype(F32)
    for d in range(1, ny):
        sum_in = sum_in + l_y[d - 1].astype(F32)
    pce[0] = sum_in.astype(BF16)
    own_in = gather(0)
    gathered(1)
    gathered(0)

    @pl.when(home != c)
    def _():
        own_in.wait_send()
        own_out.wait_send()

    for e in range(NC):
        for u in range(core_span // ROWS16):
            row = u * ROWS16
            j = next(j for j in range(per_core) if row < min(j * piece, core_span - piece) + piece)
            off = row - min(j * piece, core_span - piece)
            p, r = row // core_rows, row % core_rows
            for t, ref in enumerate((gin_ref, gout_ref)):
                ref[pl.ds(r, ROWS16), pl.ds(e * half + p * LANE, LANE)] = fin[
                    t, e * per_core + j, pl.ds(off, ROWS16), :
                ].astype(F32)

    for q in ecopies:
        q.wait_recv()
    for q in started:
        q.wait_send()


def place_outputs(enc, gin, gout, enc_to, gin_to, gout_to, sem):
    copies = []
    for i, (src, dst) in enumerate(((enc, enc_to), (gin, gin_to), (gout, gout_to))):
        copies.append(pltpu.make_async_copy(src, dst, sem.at[i]))
        copies[i].start()
    for copy in copies:
        copy.wait()


def shards(ny, nzl, frames, frame_keep, destination, ln_gain, ln_bias, w_in, w_out, upstream):
    nf, width = frames.shape
    nb = destination.shape[0]
    run = nf // nb
    rows = upstream.shape[0]
    cap = rows // (run * ny * 4)
    units = w_in.shape[1]
    half = units // NC
    own_rows = width // (ny * NZH)
    panels = half // LANE
    prow = panels * own_rows
    piece = -(-prow // (nzl * ROWS16)) * ROWS16
    per_core = nzl // NC
    nz = NZH * nzl
    ygroup = ny // NX
    nm = ygroup * 4
    grad_scale = float(nf * ny * 4 * nzl) ** (-0.5)
    quarter = rows // NX
    ysteps, zsteps = ny // 2, nz // 2
    core_rows = own_rows // NC
    dma = pltpu.SemaphoreType.DMA
    vm = pltpu.VMEM
    pairs = [2, nm, 1, 16, 2 * OPARTS * ysteps, 2 * IPARTS * zsteps, nz - 1, ny - 1, (2, nzl), 1, NX - 1, NX - 1]
    sems = []
    for i, n in enumerate(pairs):
        shape = n if isinstance(n, tuple) else (n,)
        sems += [dma(shape)] if i == 0 else [dma(shape), dma(shape)]
    vspec = pl.BlockSpec(memory_space=pltpu.VMEM)
    aspec = pl.BlockSpec(memory_space=pl.ANY)
    enc, gin, gout = pl.pallas_call(
        functools.partial(kernel, (ny, nzl, cap, run, 0.5 * grad_scale)),
        out_shape=(
            jax.ShapeDtypeStruct((rows, width), BF16),
            jax.ShapeDtypeStruct((core_rows, units), F32),
            jax.ShapeDtypeStruct((core_rows, units), F32),
        ),
        in_specs=[vspec, vspec, vspec, vspec, vspec, aspec, aspec, vspec],
        out_specs=(vspec, vspec, vspec),
        scratch_shapes=[
            vm((width, half), BF16),
            vm((half, width), BF16),
            vm((nm * ROWS16, width + LANE), BF16),
            vm((nm * ROWS16, width + LANE), BF16),
            vm((NC * rows, width + LANE), BF16),
            vm((NC * rows, width), BF16),
            vm((width, NC * rows), BF16),
            vm((NC * rows, half), F32),
            vm((width, NC * rows), BF16),
            vm((NC * rows, half), BF16),
            vm((NC * rows, half), BF16),
            vm((NZH, ny, prow, LANE), BF16),
            vm((NZH, ny, prow, LANE), BF16),
            vm((2, OPARTS, ysteps, prow * NZH // OPARTS, LANE), BF16),
            vm((2, IPARTS, zsteps, ny // IPARTS, piece, LANE), BF16),
            vm((NZH, prow, LANE), BF16),
            vm((ny, piece, LANE), BF16),
            vm((nz - 1, piece, LANE), BF16),
            vm((ny - 1, piece, LANE), BF16),
            vm((2, piece, LANE), BF16),
            vm((2, NC * per_core, piece, LANE), BF16),
            vm((rows, width), F32),
            vm((rows, width), BF16),
            vm((rows, width), BF16),
            vm((rows, width), BF16),
            vm((NX - 1, quarter, width), BF16),
        ]
        + sems,
        compiler_params=pltpu.CompilerParams(
            collective_id=0, has_side_effects=True, vmem_limit_bytes=56 * 1024 * 1024
        ),
        name="ffn_step",
    )(
        destination.reshape(1, nb),
        frame_keep,
        frames,
        ln_gain.reshape(1, width),
        ln_bias.reshape(1, width),
        w_in,
        w_out,
        upstream,
    )
    enc, gin, gout = pl.pallas_call(
        place_outputs,
        out_shape=tuple(jax.ShapeDtypeStruct(v.shape, v.dtype) for v in (enc, gin, gout)),
        in_specs=[vspec] * 3,
        out_specs=(aspec,) * 3,
        scratch_shapes=[dma((3,))],
        name="place_outputs",
    )(enc, gin, gout)
    return (enc, gin, gout.T)


def solution(mesh):
    placed = (
        P(("dp", "mp"), None),
        P(("dp", "mp")),
        P(("dp", "mp"), None),
        P(),
        P(),
        P(None, "group"),
        P("group", None),
        P(("dp", "mp"), None),
    )
    ny = mesh.shape["dp"] // (NZH * NC)
    return jax.shard_map(
        functools.partial(shards, ny, mesh.shape["mp"]),
        mesh=mesh,
        in_specs=placed,
        out_specs=(P(("dp", "mp"), None), P("dp", "group"), P("group", "dp")),
        check_vma=False,
    )
```

```python
import functools
import jax
import jax.numpy as jnp
from jax import lax
from jax.experimental import pallas as pl
from jax.experimental.pallas import tpu as pltpu
from jax.sharding import PartitionSpec as P

MESH = pl.DeviceIdType.MESH
NX = 4
NC = 2
NZH = 2
LANE = 128
ROWS16 = 16
F32 = jnp.float32
BF16 = jnp.bfloat16
I32 = jnp.int32
OPARTS = 2
IPARTS = 2


def iota(shape, axis):
    return lax.broadcasted_iota(I32, shape, axis)


def dot(a, b):
    return jnp.dot(a, b, preferred_element_type=F32)


def kernel(
    dims,
    dest_ref,
    keep_ref,
    frames_hbm,
    gain_ref,
    bias_ref,
    w_in_hbm,
    w_out_hbm,
    up_hbm,
    enc_ref,
    gin_ref,
    gout_ref,
    w_in,
    w_out,
    frames_ref,
    up_ref,
    msg,
    arr,
    tok,
    ups,
    ups_t,
    back,
    nrm_t,
    hid,
    act,
    g_out,
    g_in,
    r_out,
    r_in,
    s_out,
    s_in,
    l_z,
    l_y,
    pce,
    fin,
    p_own,
    p_oth,
    p_rcv,
    q_sum,
    q_rcv,
    w_sem,
    a_snd,
    a_rcv,
    u_snd,
    u_rcv,
    t_snd,
    t_rcv,
    o_snd,
    o_rcv,
    i_snd,
    i_rcv,
    z_snd,
    z_rcv,
    y_snd,
    y_rcv,
    f_snd,
    f_rcv,
    p_snd,
    p_rsm,
    q_snd,
    q_rsm,
    e_snd,
    e_rcv,
):
    ny, nzl, cap, run, scale = dims
    nz = NZH * nzl
    rows, width = up_ref.shape
    half = w_in.shape[1]
    slab = rows // ny
    pair_rows = cap * run
    panels = half // LANE
    own_rows = width // (ny * NZH)
    prow = panels * own_rows
    core_rows = own_rows // NC
    core_span = panels * core_rows
    per_core = nzl // NC
    piece = pce.shape[1]
    quarter = rows // NX
    ygroup = ny // NX
    mrows = msg.shape[0] // (ygroup * 4)

    dp = lax.axis_index("dp")
    y = lax.div(dp, 4)
    zh = lax.rem(lax.div(dp, 2), 2)
    c = lax.rem(dp, 2)
    zl = lax.axis_index("mp")
    x = lax.axis_index("group")
    z = zh * nzl + zl
    pc = 1 - c

    def wrap(v, n):
        return lax.rem(v + n, n)

    def at_y(v):
        return {"dp": v * 4 + zh * 2 + c}

    def at_z(v):
        return {"dp": y * 4 + lax.div(v, nzl) * 2 + c, "mp": lax.rem(v, nzl)}

    def at_x(v):
        return {"group": v}

    partner = {"dp": y * 4 + zh * 2 + pc}

    started = []

    def flush(count):
        for copy in started[:count]:
            copy.wait_send()
        del started[:count]

    def send(src, dst, snd, rcv, where):
        copy = pltpu.make_async_remote_copy(
            src_ref=src, dst_ref=dst, send_sem=snd, recv_sem=rcv, device_id=where, device_id_type=MESH
        )
        copy.start()
        started.append(copy)
        return copy

    get_w_in = pltpu.make_async_copy(w_in_hbm.at[:, pl.ds(pl.multiple_of(c * half, half), half)], w_in, w_sem.at[0])
    get_w_out = pltpu.make_async_copy(w_out_hbm.at[pl.ds(pl.multiple_of(c * half, half), half), :], w_out, w_sem.at[1])

    get_frames = pltpu.make_async_copy(frames_hbm, frames_ref, w_sem.at[2])
    get_up = pltpu.make_async_copy(up_hbm, up_ref, w_sem.at[3])
    get_frames.start()

    barrier = pltpu.get_barrier_semaphore()
    greeted = 0
    kinds = [(g, dz, dc) for g in range(ygroup) for dz in range(2) for dc in range(2)]

    def a2a_id(yy, dz, dc):
        zz = (1 - zh) if dz else zh
        cc = pc if dc else c
        return {"dp": yy * 4 + zz * 2 + cc}

    sources = []
    for g, dz, dc in kinds:
        if dz or dc:
            sources.append(a2a_id(wrap(y - x - NX * g + ny, ny), dz, dc))
    sources += [at_y(wrap(y - d, ny)) for d in range(1, ny)]
    sources += [at_z(wrap(z - d, nz)) for d in range(1, nz)]
    sources += [at_x(wrap(x - d, NX)) for d in range(1, NX)]
    sources += [{"dp": y * 4 + zh * 2 + pc, "mp": wrap(zl - d, nzl)} for d in range(1, nzl)]
    sources += [partner]
    for where in sources:
        pl.semaphore_signal(barrier, inc=1, device_id=where, device_id_type=MESH)

    get_up.start()
    get_w_out.start()
    get_w_in.start()

    nb = dest_ref.shape[1]
    nf = nb * run
    bi, bj = iota((nb, nb), 0), iota((nb, nb), 1)
    drow = jnp.broadcast_to(dest_ref[...], (nb, nb))
    dcol = jnp.sum(jnp.where(bi == bj, drow, 0), axis=1, keepdims=True)
    rank = jnp.sum(jnp.where((dcol == drow) & (bi < bj), 1, 0), axis=0, keepdims=True)
    slot = (dest_ref[...] * cap + rank).astype(F32).astype(BF16)
    spread = (iota((nb, nf), 0) == lax.div(iota((nb, nf), 1), run)).astype(F32).astype(BF16)
    slot_f = dot(jnp.broadcast_to(slot, (8, nb)), spread)[0:1, :]
    nm = len(kinds)
    mi = iota((nm * ROWS16, 1), 0)
    mk, mr = lax.div(mi, ROWS16), lax.rem(mi, ROWS16)
    mg, mdz, mdc = lax.div(mk, 4), lax.rem(lax.div(mk, 2), 2), lax.rem(mk, 2)
    my = lax.rem(y + x + NX * mg, ny)
    mzh = lax.rem(zh + mdz, 2)
    mc = lax.rem(c + mdc, 2)
    want = ((my * 4 + mzh * 2 + mc) * cap + lax.div(mr, run)).astype(F32)
    shape = (nm * ROWS16, nf)
    hit = (
        (jnp.broadcast_to(slot_f, shape) == jnp.broadcast_to(want, shape))
        & (lax.rem(iota(shape, 1), run) == jnp.broadcast_to(lax.rem(mr, run), shape))
        & (jnp.broadcast_to(mr, shape) < pair_rows)
    )
    place = jnp.where(hit, 1.0, 0.0)
    keep_row = keep_ref[...].reshape(1, nf).astype(F32)
    keep_col = jnp.sum(place * keep_row, axis=1, keepdims=True)
    get_frames.wait()
    packed = dot(place.astype(BF16), frames_ref[...])
    flags = jnp.broadcast_to(keep_col, (nm * ROWS16, LANE))
    lanes = width // LANE
    spare = jnp.zeros((mrows - (lanes + 1) * pair_rows, LANE), F32)
    for k in range(nm):
        at = slice(k * ROWS16, k * ROWS16 + pair_rows)
        parts = [packed[at, j * LANE : (j + 1) * LANE] for j in range(lanes)] + [flags[at, :], spare]
        msg[pl.ds(k * mrows, mrows), :] = jnp.concatenate(parts, axis=0).astype(BF16)
    mine = pl.ds(pl.multiple_of(c * rows, rows), rows)
    theirs = pl.ds(pl.multiple_of(pc * rows, rows), rows)

    pl.semaphore_wait(barrier, len(sources))

    a2a = []

    def a2a_send(k):
        g, dz, dc = kinds[k]
        spot = pl.ds(pl.multiple_of((g * 4 + zh * 2 + c) * mrows, ROWS16), mrows)
        part = msg.at[pl.ds(k * mrows, mrows), :]
        copy = pltpu.make_async_remote_copy(
            src_ref=part,
            dst_ref=arr.at[spot, :],
            send_sem=a_snd.at[k],
            recv_sem=a_rcv.at[k],
            device_id=a2a_id(lax.rem(y + x + NX * g, ny), dz, dc),
            device_id_type=MESH,
        )
        a2a.append(copy)
        if k:
            copy.start()
            return None
        local = pltpu.make_async_copy(part, arr.at[spot, :], a_rcv.at[k])

        @pl.when(x == 0)
        def _():
            local.start()

        @pl.when(x != 0)
        def _():
            copy.start()

        return local

    def back_of(where):
        u = ups[where, :]
        back[where, :] = lax.dot_general(u, w_out[...], (((1,), (1,)), ((), ())), preferred_element_type=F32)
        ups_t[:, where] = u.T

    locals_of = {}
    for k in range(4):
        locals_of[k] = a2a_send(k)
    local = locals_of[0]
    get_up.wait()
    ups[mine, :] = (scale * up_ref[...].astype(F32)).astype(BF16)
    ucopy = send(ups.at[mine, :], ups.at[mine, :], u_snd.at[0], u_rcv.at[0], partner)
    get_w_out.wait()
    back_of(mine)
    for k in range(4, nm):
        a2a_send(k)
    ucopy.wait_recv()
    back_of(theirs)
    get_w_in.wait()

    def rows_of(origin, g):
        ys = lax.rem(y - origin - NX * g + 2 * ny, ny)
        return tok.at[pl.ds(pl.multiple_of(c * rows + ys * slab, ROWS16), slab), :]

    def t_at(second, o, g):
        return second * 8 + o * 2 + g

    xn, xp, xo = wrap(x + 1, NX), wrap(x - 1, NX), wrap(x + 2, NX)
    origins = {0: x, 1: xn, 2: xo, 3: xp}

    def t_send(o, g, second, slot_at_receiver, tag, where):
        ref = rows_of(origins[o], g)
        return send(ref, ref, t_snd.at[tag], t_rcv.at[t_at(second, slot_at_receiver, g)], where)

    waits = {}
    for g in range(ygroup):
        for k in range(g * 4, g * 4 + 4):
            if k == 0:

                @pl.when(x == 0)
                def _():
                    local.wait()

                @pl.when(x != 0)
                def _():
                    a2a[0].wait()
            else:
                a2a[k].wait()
        got = arr[pl.ds(g * 4 * mrows, 4 * mrows), :].astype(F32)
        mine_now = rows_of(x, g)
        for j in range(lanes + 1):
            parts = [got[m * mrows + j * pair_rows : m * mrows + (j + 1) * pair_rows, :] for m in range(4)]
            mine_now[:, pl.ds(j * LANE, LANE)] = jnp.concatenate(parts, axis=0).astype(BF16)
        if g == 0:
            waits[3, g] = t_send(0, g, 0, 3, g, at_x(xn))
            waits[1, g] = t_send(0, g, 0, 1, 2 + g, at_x(xp))
        else:
            waits[1, g] = t_send(0, g, 0, 1, 2 + g, at_x(xp))
            waits[3, g] = t_send(0, g, 0, 3, g, at_x(xn))
        waits["c", 0, g] = t_send(0, g, 1, 0, 4 + g, partner)
    waits[3, 0].wait_recv()
    waits[2, 0] = t_send(3, 0, 0, 2, 6, at_x(xn))
    waits["c", 3, 0] = t_send(3, 0, 1, 3, 8, partner)
    waits[1, 1].wait_recv()
    waits[2, 1] = t_send(1, 1, 0, 2, 7, at_x(xp))
    waits["c", 1, 1] = t_send(1, 1, 1, 1, 9, partner)
    waits[1, 0].wait_recv()
    waits["c", 1, 0] = t_send(1, 0, 1, 1, 11, partner)
    waits[3, 1].wait_recv()
    waits["c", 3, 1] = t_send(3, 1, 1, 3, 10, partner)
    for g in range(ygroup):
        waits[2, g].wait_recv()
        waits["c", 2, g] = t_send(2, g, 1, 2, 12 + g, partner)
    for o in (0, 3, 1, 2):
        for g in range(ygroup):
            waits["c", o, g].wait_recv()

    step_rows = LANE
    for t in range(2 * rows // step_rows):
        at = pl.ds(t * step_rows, step_rows)
        feat = tok[at, :width].astype(F32)
        live = tok[at, width:][:, 0:1].astype(F32)
        mean = jnp.mean(feat, axis=1, keepdims=True)
        cen = feat - mean
        var = jnp.mean(cen * cen, axis=1, keepdims=True)
        norm = (cen * lax.rsqrt(var + 1e-05) * gain_ref[...] + bias_ref[...]).astype(BF16)
        nrm_t[:, at] = norm.T
        pre = dot(norm, w_in[...])
        sig = jax.nn.sigmoid(pre)
        hid[at, :] = (live * (pre * sig)).astype(BF16)
        act[at, :] = (live * back[at, :] * (sig + pre * sig * (1.0 - sig))).astype(BF16)

    def gradient(left, right, out):
        block = 2 * LANE
        for b in range(width // block):
            val = dot(left[pl.ds(b * block, block), :], right[...]).astype(BF16)
            for u in range(block // own_rows):
                unit = b * (block // own_rows) + u
                for e in range(NC):
                    for p in range(panels):
                        row = u * own_rows + e * core_rows
                        out[unit % NZH, unit // NZH, pl.ds((e * panels + p) * core_rows, core_rows), :] = val[
                            row : row + core_rows, p * LANE : (p + 1) * LANE
                        ]

    def start_of(j):
        core_at = lax.div(j, per_core)
        inside = jnp.minimum(lax.rem(j, per_core) * piece, core_span - piece)
        return pl.multiple_of(core_at * core_span + inside, ROWS16)

    ysteps = ny // 2
    ochain = {}
    ocut = OPARTS // NZH
    orows = prow // ocut

    def o_own(q, v):
        return g_out.at[q // ocut, v, pl.ds(q % ocut * orows, orows), :]

    def o_step(phase, s):
        for d in range(2):
            sign = 1 - 2 * d
            for q in range(OPARTS):
                if (d == q % 2) != (phase == 0):
                    continue
                first = 1 + phase
                own = o_own(q, wrap(y + sign * (ysteps + 1 - s), ny))
                if s == first:
                    src = own
                else:
                    ochain[d, q, s - 1].wait_recv()
                    src = r_out.at[d, q, s - 2]
                    src[...] = (src[...].astype(F32) + own[...].astype(F32)).astype(BF16)
                tag = (d * OPARTS + q) * ysteps + s - 1
                ochain[d, q, s] = send(
                    src, r_out.at[d, q, s - 1], o_snd.at[tag], o_rcv.at[tag], at_y(wrap(y + sign, ny))
                )

    zsteps = nz // 2
    ichain = {}
    hy = ny // IPARTS

    def i_own(q, v):
        return g_in.at[lax.div(v, nzl), pl.ds(q * hy, hy), pl.ds(start_of(lax.rem(v, nzl)), piece), :]

    def i_step(phase, s):
        for d in range(2):
            sign = 1 - 2 * d
            for q in range(IPARTS):
                if (d == q % 2) != (phase == 0):
                    continue
                first = 1 + phase
                own = i_own(q, wrap(z + sign * (zsteps + 1 - s), nz))
                if s == first:
                    src = own
                else:
                    ichain[d, q, s - 1].wait_recv()
                    src = r_in.at[d, q, s - 2]
                    src[...] = (src[...].astype(F32) + own[...].astype(F32)).astype(BF16)
                tag = (d * IPARTS + q) * zsteps + s - 1
                ichain[d, q, s] = send(
                    src, r_in.at[d, q, s - 1], i_snd.at[tag], i_rcv.at[tag], at_z(wrap(z + sign, nz))
                )

    gradient(nrm_t, act, g_in)
    i_step(0, 1)
    gradient(ups_t, hid, g_out)
    o_step(0, 1)
    i_step(1, 2)
    p_oth[...] = dot(hid[theirs, :], w_out[...]).astype(BF16)
    o_step(1, 2)
    pcopy = send(p_oth, p_rcv, p_snd.at[0], p_rsm.at[0], partner)
    i_step(0, 2)
    o_step(0, 2)
    p_own[...] = dot(hid[mine, :], w_out[...])
    i_step(1, 3)
    o_step(1, 3)
    i_step(0, 3)
    o_step(0, 3)
    i_step(1, 4)
    o_step(1, 4)
    pcopy.wait_recv()
    q_sum[...] = (p_own[...] + p_rcv[...].astype(F32)).astype(BF16)
    qcopies = []
    for d in range(1, NX):
        to = wrap(x + d, NX)
        part = q_sum.at[pl.ds(pl.multiple_of(to * quarter, quarter), quarter), :]
        qcopies.append(send(part, q_rcv.at[d - 1], q_snd.at[d - 1], q_rsm.at[d - 1], at_x(to)))
    i_step(0, 4)
    o_step(0, 4)
    i_step(1, 5)
    i_step(0, 5)

    zcopies = []
    for q in range(OPARTS):
        ochain[0, q, ysteps].wait_recv()
        ochain[1, q, ysteps].wait_recv()
        s_out[q // ocut, pl.ds(q % ocut * orows, orows), :] = (
            o_own(q, y)[...].astype(F32)
            + r_out[0, q, ysteps - 1].astype(F32)
            + r_out[1, q, ysteps - 1].astype(F32)
        ).astype(BF16)
    for d in range(1, nz):
        to = wrap(z + d, nz)
        part = s_out.at[lax.div(to, nzl), pl.ds(start_of(lax.rem(to, nzl)), piece), :]
        zcopies.append(send(part, l_z.at[d - 1], z_snd.at[d - 1], z_rcv.at[d - 1], at_z(to)))
    i_step(1, 6)
    i_step(0, 6)

    gone = len(started)
    for q in range(IPARTS):
        ichain[0, q, zsteps].wait_recv()
        ichain[1, q, zsteps].wait_recv()
        s_in[pl.ds(q * hy, hy)] = (
            i_own(q, z)[...].astype(F32)
            + r_in[0, q, zsteps - 1].astype(F32)
            + r_in[1, q, zsteps - 1].astype(F32)
        ).astype(BF16)
    ycopies = []
    for d in range(1, ny):
        to = wrap(y + d, ny)
        ycopies.append(send(s_in.at[to], l_y.at[d - 1], y_snd.at[d - 1], y_rcv.at[d - 1], at_y(to)))

    home = lax.div(zl, per_core)
    spot = c * per_core + lax.rem(zl, per_core)

    def gather(t):
        def base(d):
            return pltpu.make_async_remote_copy(
                src_ref=pce.at[t],
                dst_ref=fin.at[t, spot],
                send_sem=f_snd.at[t, d],
                recv_sem=f_rcv.at[t, spot],
                device_id={"dp": y * 4 + zh * 2 + home, "mp": wrap(zl + d, nzl)},
                device_id_type=MESH,
            )

        @pl.when(home == c)
        def _():
            pltpu.make_async_copy(pce.at[t], fin.at[t, spot], f_rcv.at[t, spot]).start()

        @pl.when(home != c)
        def _():
            base(0).start()

        for d in range(1, nzl):
            copy = base(d)
            copy.start()
            started.append(copy)
        return base(0)

    def gathered(t):
        for slot in range(NC * per_core):
            pltpu.make_async_copy(pce.at[t], fin.at[t, slot], f_rcv.at[t, slot]).wait()

    flush(gone)
    for q in zcopies:
        q.wait_recv()
    sum_out = s_out[zh, pl.ds(start_of(zl), piece), :].astype(F32)
    for d in range(1, nz):
        sum_out = sum_out + l_z[d - 1].astype(F32)
    pce[1] = sum_out.astype(BF16)
    own_out = gather(1)
    for q in qcopies:
        q.wait_recv()
    xrows = pl.ds(pl.multiple_of(x * quarter, quarter), quarter)
    total = q_sum[xrows, :].astype(F32)
    for d in range(1, NX):
        total = total + q_rcv[d - 1].astype(F32)
    trows = pl.ds(pl.multiple_of(c * rows + x * quarter, ROWS16), quarter)
    feat = tok[trows, :width].astype(F32)
    live = tok[trows, width:][:, 0:1].astype(F32)
    enc_ref[xrows, :] = (live * (feat + 0.5 * total)).astype(BF16)
    ecopies = []
    for d in range(1, NX):
        part = enc_ref.at[xrows, :]
        ecopies.append(send(part, part, e_snd.at[d - 1], e_rcv.at[d - 1], at_x(wrap(x + d, NX))))

    flush(len(started) - (nzl - 1))
    for q in ycopies:
        q.wait_recv()
    sum_in = s_in[y].astype(F32)
    for d in range(1, ny):
        sum_in = sum_in + l_y[d - 1].astype(F32)
    pce[0] = sum_in.astype(BF16)
    own_in = gather(0)
    gathered(1)
    gathered(0)

    @pl.when(home != c)
    def _():
        own_in.wait_send()
        own_out.wait_send()

    for e in range(NC):
        for u in range(core_span // ROWS16):
            row = u * ROWS16
            j = next(j for j in range(per_core) if row < min(j * piece, core_span - piece) + piece)
            off = row - min(j * piece, core_span - piece)
            p, r = row // core_rows, row % core_rows
            for t, ref in enumerate((gin_ref, gout_ref)):
                ref[pl.ds(r, ROWS16), pl.ds(e * half + p * LANE, LANE)] = fin[
                    t, e * per_core + j, pl.ds(off, ROWS16), :
                ].astype(F32)

    for q in ecopies:
        q.wait_recv()
    for q in started:
        q.wait_send()


def place_outputs(enc, gin, gout, enc_to, gin_to, gout_to, sem):
    copies = []
    for i, (src, dst) in enumerate(((enc, enc_to), (gin, gin_to), (gout, gout_to))):
        copies.append(pltpu.make_async_copy(src, dst, sem.at[i]))
        copies[i].start()
    for copy in copies:
        copy.wait()


def shards(ny, nzl, frames, frame_keep, destination, ln_gain, ln_bias, w_in, w_out, upstream):
    nf, width = frames.shape
    nb = destination.shape[0]
    run = nf // nb
    rows = upstream.shape[0]
    cap = rows // (run * ny * 4)
    units = w_in.shape[1]
    half = units // NC
    own_rows = width // (ny * NZH)
    panels = half // LANE
    prow = panels * own_rows
    piece = -(-prow // (nzl * ROWS16)) * ROWS16
    per_core = nzl // NC
    nz = NZH * nzl
    ygroup = ny // NX
    nm = ygroup * 4
    mrows = -(-(width // LANE + 1) * cap * run // ROWS16) * ROWS16
    grad_scale = float(nf * ny * 4 * nzl) ** (-0.5)
    quarter = rows // NX
    ysteps, zsteps = ny // 2, nz // 2
    core_rows = own_rows // NC
    dma = pltpu.SemaphoreType.DMA
    vm = pltpu.VMEM
    pairs = [4, nm, 1, 16, 2 * OPARTS * ysteps, 2 * IPARTS * zsteps, nz - 1, ny - 1, (2, nzl), 1, NX - 1, NX - 1]
    sems = []
    for i, n in enumerate(pairs):
        shape = n if isinstance(n, tuple) else (n,)
        sems += [dma(shape)] if i == 0 else [dma(shape), dma(shape)]
    vspec = pl.BlockSpec(memory_space=pltpu.VMEM)
    aspec = pl.BlockSpec(memory_space=pl.ANY)
    enc, gin, gout = pl.pallas_call(
        functools.partial(kernel, (ny, nzl, cap, run, 0.5 * grad_scale)),
        out_shape=(
            jax.ShapeDtypeStruct((rows, width), BF16),
            jax.ShapeDtypeStruct((core_rows, units), F32),
            jax.ShapeDtypeStruct((core_rows, units), F32),
        ),
        in_specs=[vspec, vspec, aspec, vspec, vspec, aspec, aspec, aspec],
        out_specs=(vspec, vspec, vspec),
        scratch_shapes=[
            vm((width, half), BF16),
            vm((half, width), BF16),
            vm((nf, width), BF16),
            vm((rows, width), BF16),
            vm((nm * mrows, LANE), BF16),
            vm((nm * mrows, LANE), BF16),
            vm((NC * rows, width + LANE), BF16),
            vm((NC * rows, width), BF16),
            vm((width, NC * rows), BF16),
            vm((NC * rows, half), F32),
            vm((width, NC * rows), BF16),
            vm((NC * rows, half), BF16),
            vm((NC * rows, half), BF16),
            vm((NZH, ny, prow, LANE), BF16),
            vm((NZH, ny, prow, LANE), BF16),
            vm((2, OPARTS, ysteps, prow * NZH // OPARTS, LANE), BF16),
            vm((2, IPARTS, zsteps, ny // IPARTS, piece, LANE), BF16),
            vm((NZH, prow, LANE), BF16),
            vm((ny, piece, LANE), BF16),
            vm((nz - 1, piece, LANE), BF16),
            vm((ny - 1, piece, LANE), BF16),
            vm((2, piece, LANE), BF16),
            vm((2, NC * per_core, piece, LANE), BF16),
            vm((rows, width), F32),
            vm((rows, width), BF16),
            vm((rows, width), BF16),
            vm((rows, width), BF16),
            vm((NX - 1, quarter, width), BF16),
        ]
        + sems,
        compiler_params=pltpu.CompilerParams(
            collective_id=0, has_side_effects=True, vmem_limit_bytes=56 * 1024 * 1024
        ),
        name="ffn_step",
    )(
        destination.reshape(1, nb),
        frame_keep,
        frames,
        ln_gain.reshape(1, width),
        ln_bias.reshape(1, width),
        w_in,
        w_out,
        upstream,
    )
    enc, gin, gout = pl.pallas_call(
        place_outputs,
        out_shape=tuple(jax.ShapeDtypeStruct(v.shape, v.dtype) for v in (enc, gin, gout)),
        in_specs=[vspec] * 3,
        out_specs=(aspec,) * 3,
        scratch_shapes=[dma((3,))],
        name="place_outputs",
    )(enc, gin, gout)
    return (enc, gin, gout.T)


def solution(mesh):
    placed = (
        P(("dp", "mp"), None),
        P(("dp", "mp")),
        P(("dp", "mp"), None),
        P(),
        P(),
        P(None, "group"),
        P("group", None),
        P(("dp", "mp"), None),
    )
    ny = mesh.shape["dp"] // (NZH * NC)
    return jax.shard_map(
        functools.partial(shards, ny, mesh.shape["mp"]),
        mesh=mesh,
        in_specs=placed,
        out_specs=(P(("dp", "mp"), None), P("dp", "group"), P("group", "dp")),
        check_vma=False,
    )
```

```python
import functools
import jax
import jax.numpy as jnp
from jax import lax
from jax.experimental import pallas as pl
from jax.experimental.pallas import tpu as pltpu
from jax.sharding import PartitionSpec as P

MESH = pl.DeviceIdType.MESH
NX = 4
NC = 2
NZH = 2
LANE = 128
ROWS16 = 16
F32 = jnp.float32
BF16 = jnp.bfloat16
I32 = jnp.int32
OPARTS = 2
IPARTS = 2


def iota(shape, axis):
    return lax.broadcasted_iota(I32, shape, axis)


def dot(a, b):
    return jnp.dot(a, b, preferred_element_type=F32)


def kernel(
    dims,
    dest_ref,
    keep_ref,
    frames_hbm,
    gain_ref,
    bias_ref,
    w_in_hbm,
    w_out_hbm,
    up_hbm,
    enc_ref,
    gin_ref,
    gout_ref,
    w_in,
    w_out,
    frames_ref,
    up_ref,
    msg,
    arr,
    tok,
    ups,
    ups_t,
    back,
    nrm_t,
    hid,
    act,
    g_out,
    g_in,
    r_out,
    r_in,
    s_out,
    s_in,
    l_z,
    l_y,
    pce,
    fin,
    p_own,
    p_oth,
    p_rcv,
    q_sum,
    q_rcv,
    w_sem,
    a_snd,
    a_rcv,
    u_snd,
    u_rcv,
    t_snd,
    t_rcv,
    o_snd,
    o_rcv,
    i_snd,
    i_rcv,
    z_snd,
    z_rcv,
    y_snd,
    y_rcv,
    f_snd,
    f_rcv,
    p_snd,
    p_rsm,
    q_snd,
    q_rsm,
    e_snd,
    e_rcv,
):
    ny, nzl, cap, run, scale = dims
    nz = NZH * nzl
    rows, width = up_ref.shape
    half = w_in.shape[1]
    slab = rows // ny
    pair_rows = cap * run
    panels = half // LANE
    own_rows = width // (ny * NZH)
    prow = panels * own_rows
    core_rows = own_rows // NC
    core_span = panels * core_rows
    per_core = nzl // NC
    piece = pce.shape[1]
    quarter = rows // NX
    ygroup = ny // NX
    mrows = msg.shape[0] // (ygroup * 4)

    dp = lax.axis_index("dp")
    y = lax.div(dp, 4)
    zh = lax.rem(lax.div(dp, 2), 2)
    c = lax.rem(dp, 2)
    zl = lax.axis_index("mp")
    x = lax.axis_index("group")
    z = zh * nzl + zl
    pc = 1 - c

    def wrap(v, n):
        return lax.rem(v + n, n)

    def at_y(v):
        return {"dp": v * 4 + zh * 2 + c}

    def at_z(v):
        return {"dp": y * 4 + lax.div(v, nzl) * 2 + c, "mp": lax.rem(v, nzl)}

    def at_x(v):
        return {"group": v}

    partner = {"dp": y * 4 + zh * 2 + pc}

    started = []

    def flush(count):
        for copy in started[:count]:
            copy.wait_send()
        del started[:count]

    def send(src, dst, snd, rcv, where):
        copy = pltpu.make_async_remote_copy(
            src_ref=src, dst_ref=dst, send_sem=snd, recv_sem=rcv, device_id=where, device_id_type=MESH
        )
        copy.start()
        started.append(copy)
        return copy

    get_w_in = pltpu.make_async_copy(w_in_hbm.at[:, pl.ds(pl.multiple_of(c * half, half), half)], w_in, w_sem.at[0])
    get_w_out = pltpu.make_async_copy(w_out_hbm.at[pl.ds(pl.multiple_of(c * half, half), half), :], w_out, w_sem.at[1])

    get_frames = pltpu.make_async_copy(frames_hbm, frames_ref, w_sem.at[2])
    get_up = pltpu.make_async_copy(up_hbm, up_ref, w_sem.at[3])
    get_frames.start()

    barrier = pltpu.get_barrier_semaphore()
    greeted = 0
    kinds = [(g, dz, dc) for g in range(ygroup) for dz in range(2) for dc in range(2)]

    def a2a_id(yy, dz, dc):
        zz = (1 - zh) if dz else zh
        cc = pc if dc else c
        return {"dp": yy * 4 + zz * 2 + cc}

    sources = []
    for g, dz, dc in kinds:
        if dz or dc:
            sources.append(a2a_id(wrap(y - x - NX * g + ny, ny), dz, dc))
    sources += [at_y(wrap(y - d, ny)) for d in range(1, ny)]
    sources += [at_z(wrap(z - d, nz)) for d in range(1, nz)]
    sources += [at_x(wrap(x - d, NX)) for d in range(1, NX)]
    sources += [{"dp": y * 4 + zh * 2 + pc, "mp": wrap(zl - d, nzl)} for d in range(1, nzl)]
    sources += [partner]
    for where in sources:
        pl.semaphore_signal(barrier, inc=1, device_id=where, device_id_type=MESH)

    get_up.start()
    get_w_out.start()
    get_w_in.start()

    nb = dest_ref.shape[1]
    nf = nb * run
    bi, bj = iota((nb, nb), 0), iota((nb, nb), 1)
    drow = jnp.broadcast_to(dest_ref[...], (nb, nb))
    dcol = jnp.sum(jnp.where(bi == bj, drow, 0), axis=1, keepdims=True)
    rank = jnp.sum(jnp.where((dcol == drow) & (bi < bj), 1, 0), axis=0, keepdims=True)
    slot = (dest_ref[...] * cap + rank).astype(F32).astype(BF16)
    spread = (iota((nb, nf), 0) == lax.div(iota((nb, nf), 1), run)).astype(F32).astype(BF16)
    slot_f = dot(jnp.broadcast_to(slot, (8, nb)), spread)[0:1, :]
    nm = len(kinds)
    mi = iota((nm * ROWS16, 1), 0)
    mk, mr = lax.div(mi, ROWS16), lax.rem(mi, ROWS16)
    mg, mdz, mdc = lax.div(mk, 4), lax.rem(lax.div(mk, 2), 2), lax.rem(mk, 2)
    my = lax.rem(y + x + NX * mg, ny)
    mzh = lax.rem(zh + mdz, 2)
    mc = lax.rem(c + mdc, 2)
    want = ((my * 4 + mzh * 2 + mc) * cap + lax.div(mr, run)).astype(F32)
    shape = (nm * ROWS16, nf)
    hit = (
        (jnp.broadcast_to(slot_f, shape) == jnp.broadcast_to(want, shape))
        & (lax.rem(iota(shape, 1), run) == jnp.broadcast_to(lax.rem(mr, run), shape))
        & (jnp.broadcast_to(mr, shape) < pair_rows)
    )
    place = jnp.where(hit, 1.0, 0.0)
    keep_row = keep_ref[...].reshape(1, nf).astype(F32)
    keep_col = jnp.sum(place * keep_row, axis=1, keepdims=True)
    get_frames.wait()
    packed = dot(place.astype(BF16), frames_ref[...])
    flags = jnp.broadcast_to(keep_col, (nm * ROWS16, LANE))
    lanes = width // LANE
    spare = jnp.zeros((mrows - (lanes + 1) * pair_rows, LANE), F32)
    for k in range(nm):
        at = slice(k * ROWS16, k * ROWS16 + pair_rows)
        parts = [packed[at, j * LANE : (j + 1) * LANE] for j in range(lanes)] + [flags[at, :], spare]
        msg[pl.ds(k * mrows, mrows), :] = jnp.concatenate(parts, axis=0).astype(BF16)
    mine = pl.ds(pl.multiple_of(c * rows, rows), rows)
    theirs = pl.ds(pl.multiple_of(pc * rows, rows), rows)

    pl.semaphore_wait(barrier, len(sources))

    a2a = []

    def a2a_send(k):
        g, dz, dc = kinds[k]
        spot = pl.ds(pl.multiple_of((g * 4 + zh * 2 + c) * mrows, ROWS16), mrows)
        part = msg.at[pl.ds(k * mrows, mrows), :]
        copy = pltpu.make_async_remote_copy(
            src_ref=part,
            dst_ref=arr.at[spot, :],
            send_sem=a_snd.at[k],
            recv_sem=a_rcv.at[k],
            device_id=a2a_id(lax.rem(y + x + NX * g, ny), dz, dc),
            device_id_type=MESH,
        )
        a2a.append(copy)
        if k:
            copy.start()
            return None
        local = pltpu.make_async_copy(part, arr.at[spot, :], a_rcv.at[k])

        @pl.when(x == 0)
        def _():
            local.start()

        @pl.when(x != 0)
        def _():
            copy.start()

        return local

    def back_of(where):
        u = ups[where, :]
        back[where, :] = lax.dot_general(u, w_out[...], (((1,), (1,)), ((), ())), preferred_element_type=F32)
        ups_t[:, where] = u.T

    locals_of = {}
    for k in range(4):
        locals_of[k] = a2a_send(k)
    local = locals_of[0]
    get_up.wait()
    ups[mine, :] = (scale * up_ref[...].astype(F32)).astype(BF16)
    ucopy = send(ups.at[mine, :], ups.at[mine, :], u_snd.at[0], u_rcv.at[0], partner)
    get_w_out.wait()
    back_of(mine)
    for k in range(4, nm):
        a2a_send(k)
    ucopy.wait_recv()
    back_of(theirs)
    get_w_in.wait()

    def rows_of(origin, g):
        ys = lax.rem(y - origin - NX * g + 2 * ny, ny)
        return tok.at[pl.ds(pl.multiple_of(c * rows + ys * slab, ROWS16), slab), :]

    def t_at(second, o, g):
        return second * 8 + o * 2 + g

    xn, xp, xo = wrap(x + 1, NX), wrap(x - 1, NX), wrap(x + 2, NX)
    origins = {0: x, 1: xn, 2: xo, 3: xp}

    def t_send(o, g, second, slot_at_receiver, tag, where):
        ref = rows_of(origins[o], g)
        return send(ref, ref, t_snd.at[tag], t_rcv.at[t_at(second, slot_at_receiver, g)], where)

    waits = {}
    for g in range(ygroup):
        for k in range(g * 4, g * 4 + 4):
            if k == 0:

                @pl.when(x == 0)
                def _():
                    local.wait()

                @pl.when(x != 0)
                def _():
                    a2a[0].wait()
            else:
                a2a[k].wait()
        got = arr[pl.ds(g * 4 * mrows, 4 * mrows), :].astype(F32)
        mine_now = rows_of(x, g)
        for j in range(lanes + 1):
            parts = [got[m * mrows + j * pair_rows : m * mrows + (j + 1) * pair_rows, :] for m in range(4)]
            mine_now[:, pl.ds(j * LANE, LANE)] = jnp.concatenate(parts, axis=0).astype(BF16)
        if g == 0:
            waits[3, g] = t_send(0, g, 0, 3, g, at_x(xn))
            waits[1, g] = t_send(0, g, 0, 1, 2 + g, at_x(xp))
        else:
            waits[1, g] = t_send(0, g, 0, 1, 2 + g, at_x(xp))
            waits[3, g] = t_send(0, g, 0, 3, g, at_x(xn))
        waits["c", 0, g] = t_send(0, g, 1, 0, 4 + g, partner)
    waits[3, 0].wait_recv()
    waits[2, 0] = t_send(3, 0, 0, 2, 6, at_x(xn))
    waits["c", 3, 0] = t_send(3, 0, 1, 3, 8, partner)
    waits[1, 1].wait_recv()
    waits[2, 1] = t_send(1, 1, 0, 2, 7, at_x(xp))
    waits["c", 1, 1] = t_send(1, 1, 1, 1, 9, partner)
    waits[1, 0].wait_recv()
    waits["c", 1, 0] = t_send(1, 0, 1, 1, 11, partner)
    waits[3, 1].wait_recv()
    waits["c", 3, 1] = t_send(3, 1, 1, 3, 10, partner)
    for g in range(ygroup):
        waits[2, g].wait_recv()
        waits["c", 2, g] = t_send(2, g, 1, 2, 12 + g, partner)
    step_rows = LANE

    def forward(begin):
        at = pl.ds(pl.multiple_of(begin, step_rows), step_rows)
        feat = tok[at, :width].astype(F32)
        live = tok[at, width:][:, 0:1].astype(F32)
        mean = jnp.mean(feat, axis=1, keepdims=True)
        cen = feat - mean
        var = jnp.mean(cen * cen, axis=1, keepdims=True)
        norm = (cen * lax.rsqrt(var + 1e-05) * gain_ref[...] + bias_ref[...]).astype(BF16)
        nrm_t[:, at] = norm.T
        pre = dot(norm, w_in[...])
        sig = jax.nn.sigmoid(pre)
        hid[at, :] = (live * (pre * sig)).astype(BF16)
        act[at, :] = (live * back[at, :] * (sig + pre * sig * (1.0 - sig))).astype(BF16)

    for t in range(rows // step_rows):
        forward(c * rows + t * step_rows)
    for o in (0, 3, 1, 2):
        for g in range(ygroup):
            waits["c", o, g].wait_recv()
    for t in range(rows // step_rows):
        forward(pc * rows + t * step_rows)

    def gradient(left, right, out):
        block = 2 * LANE
        for b in range(width // block):
            val = dot(left[pl.ds(b * block, block), :], right[...]).astype(BF16)
            for u in range(block // own_rows):
                unit = b * (block // own_rows) + u
                for e in range(NC):
                    for p in range(panels):
                        row = u * own_rows + e * core_rows
                        out[unit % NZH, unit // NZH, pl.ds((e * panels + p) * core_rows, core_rows), :] = val[
                            row : row + core_rows, p * LANE : (p + 1) * LANE
                        ]

    def start_of(j):
        core_at = lax.div(j, per_core)
        inside = jnp.minimum(lax.rem(j, per_core) * piece, core_span - piece)
        return pl.multiple_of(core_at * core_span + inside, ROWS16)

    ysteps = ny // 2
    ochain = {}
    ocut = OPARTS // NZH
    orows = prow // ocut

    def o_own(q, v):
        return g_out.at[q // ocut, v, pl.ds(q % ocut * orows, orows), :]

    def o_step(phase, s):
        for d in range(2):
            sign = 1 - 2 * d
            for q in range(OPARTS):
                if (d == q % 2) != (phase == 0):
                    continue
                first = 1 + phase
                own = o_own(q, wrap(y + sign * (ysteps + 1 - s), ny))
                if s == first:
                    src = own
                else:
                    ochain[d, q, s - 1].wait_recv()
                    src = r_out.at[d, q, s - 2]
                    src[...] = (src[...].astype(F32) + own[...].astype(F32)).astype(BF16)
                tag = (d * OPARTS + q) * ysteps + s - 1
                ochain[d, q, s] = send(
                    src, r_out.at[d, q, s - 1], o_snd.at[tag], o_rcv.at[tag], at_y(wrap(y + sign, ny))
                )

    zsteps = nz // 2
    ichain = {}
    hy = ny // IPARTS

    def i_own(q, v):
        return g_in.at[lax.div(v, nzl), pl.ds(q * hy, hy), pl.ds(start_of(lax.rem(v, nzl)), piece), :]

    def i_step(phase, s):
        for d in range(2):
            sign = 1 - 2 * d
            for q in range(IPARTS):
                if (d == q % 2) != (phase == 0):
                    continue
                first = 1 + phase
                own = i_own(q, wrap(z + sign * (zsteps + 1 - s), nz))
                if s == first:
                    src = own
                else:
                    ichain[d, q, s - 1].wait_recv()
                    src = r_in.at[d, q, s - 2]
                    src[...] = (src[...].astype(F32) + own[...].astype(F32)).astype(BF16)
                tag = (d * IPARTS + q) * zsteps + s - 1
                ichain[d, q, s] = send(
                    src, r_in.at[d, q, s - 1], i_snd.at[tag], i_rcv.at[tag], at_z(wrap(z + sign, nz))
                )

    gradient(nrm_t, act, g_in)
    i_step(0, 1)
    gradient(ups_t, hid, g_out)
    o_step(0, 1)
    i_step(1, 2)
    p_oth[...] = dot(hid[theirs, :], w_out[...]).astype(BF16)
    o_step(1, 2)
    pcopy = send(p_oth, p_rcv, p_snd.at[0], p_rsm.at[0], partner)
    i_step(0, 2)
    o_step(0, 2)
    p_own[...] = dot(hid[mine, :], w_out[...])
    i_step(1, 3)
    o_step(1, 3)
    i_step(0, 3)
    o_step(0, 3)
    i_step(1, 4)
    o_step(1, 4)
    pcopy.wait_recv()
    q_sum[...] = (p_own[...] + p_rcv[...].astype(F32)).astype(BF16)
    qcopies = []
    for d in range(1, NX):
        to = wrap(x + d, NX)
        part = q_sum.at[pl.ds(pl.multiple_of(to * quarter, quarter), quarter), :]
        qcopies.append(send(part, q_rcv.at[d - 1], q_snd.at[d - 1], q_rsm.at[d - 1], at_x(to)))
    i_step(0, 4)
    o_step(0, 4)
    i_step(1, 5)
    i_step(0, 5)

    zcopies = []
    for q in range(OPARTS):
        ochain[0, q, ysteps].wait_recv()
        ochain[1, q, ysteps].wait_recv()
        s_out[q // ocut, pl.ds(q % ocut * orows, orows), :] = (
            o_own(q, y)[...].astype(F32)
            + r_out[0, q, ysteps - 1].astype(F32)
            + r_out[1, q, ysteps - 1].astype(F32)
        ).astype(BF16)
    for d in range(1, nz):
        to = wrap(z + d, nz)
        part = s_out.at[lax.div(to, nzl), pl.ds(start_of(lax.rem(to, nzl)), piece), :]
        zcopies.append(send(part, l_z.at[d - 1], z_snd.at[d - 1], z_rcv.at[d - 1], at_z(to)))
    i_step(1, 6)
    i_step(0, 6)

    gone = len(started)
    for q in range(IPARTS):
        ichain[0, q, zsteps].wait_recv()
        ichain[1, q, zsteps].wait_recv()
        s_in[pl.ds(q * hy, hy)] = (
            i_own(q, z)[...].astype(F32)
            + r_in[0, q, zsteps - 1].astype(F32)
            + r_in[1, q, zsteps - 1].astype(F32)
        ).astype(BF16)
    ycopies = []
    for d in range(1, ny):
        to = wrap(y + d, ny)
        ycopies.append(send(s_in.at[to], l_y.at[d - 1], y_snd.at[d - 1], y_rcv.at[d - 1], at_y(to)))

    home = lax.div(zl, per_core)
    spot = c * per_core + lax.rem(zl, per_core)

    def gather(t):
        def base(d):
            return pltpu.make_async_remote_copy(
                src_ref=pce.at[t],
                dst_ref=fin.at[t, spot],
                send_sem=f_snd.at[t, d],
                recv_sem=f_rcv.at[t, spot],
                device_id={"dp": y * 4 + zh * 2 + home, "mp": wrap(zl + d, nzl)},
                device_id_type=MESH,
            )

        @pl.when(home == c)
        def _():
            pltpu.make_async_copy(pce.at[t], fin.at[t, spot], f_rcv.at[t, spot]).start()

        @pl.when(home != c)
        def _():
            base(0).start()

        for d in range(1, nzl):
            copy = base(d)
            copy.start()
            started.append(copy)
        return base(0)

    def gathered(t):
        for slot in range(NC * per_core):
            pltpu.make_async_copy(pce.at[t], fin.at[t, slot], f_rcv.at[t, slot]).wait()

    flush(gone)
    for q in zcopies:
        q.wait_recv()
    sum_out = s_out[zh, pl.ds(start_of(zl), piece), :].astype(F32)
    for d in range(1, nz):
        sum_out = sum_out + l_z[d - 1].astype(F32)
    pce[1] = sum_out.astype(BF16)
    own_out = gather(1)
    for q in qcopies:
        q.wait_recv()
    xrows = pl.ds(pl.multiple_of(x * quarter, quarter), quarter)
    total = q_sum[xrows, :].astype(F32)
    for d in range(1, NX):
        total = total + q_rcv[d - 1].astype(F32)
    trows = pl.ds(pl.multiple_of(c * rows + x * quarter, ROWS16), quarter)
    feat = tok[trows, :width].astype(F32)
    live = tok[trows, width:][:, 0:1].astype(F32)
    enc_ref[xrows, :] = (live * (feat + 0.5 * total)).astype(BF16)
    ecopies = []
    for d in range(1, NX):
        part = enc_ref.at[xrows, :]
        ecopies.append(send(part, part, e_snd.at[d - 1], e_rcv.at[d - 1], at_x(wrap(x + d, NX))))

    flush(len(started) - (nzl - 1))
    for q in ycopies:
        q.wait_recv()
    sum_in = s_in[y].astype(F32)
    for d in range(1, ny):
        sum_in = sum_in + l_y[d - 1].astype(F32)
    pce[0] = sum_in.astype(BF16)
    own_in = gather(0)
    gathered(1)
    gathered(0)

    @pl.when(home != c)
    def _():
        own_in.wait_send()
        own_out.wait_send()

    for e in range(NC):
        for u in range(core_span // ROWS16):
            row = u * ROWS16
            j = next(j for j in range(per_core) if row < min(j * piece, core_span - piece) + piece)
            off = row - min(j * piece, core_span - piece)
            p, r = row // core_rows, row % core_rows
            for t, ref in enumerate((gin_ref, gout_ref)):
                ref[pl.ds(r, ROWS16), pl.ds(e * half + p * LANE, LANE)] = fin[
                    t, e * per_core + j, pl.ds(off, ROWS16), :
                ].astype(F32)

    for q in ecopies:
        q.wait_recv()
    for q in started:
        q.wait_send()


def place_outputs(enc, gin, gout, enc_to, gin_to, gout_to, sem):
    copies = []
    for i, (src, dst) in enumerate(((enc, enc_to), (gin, gin_to), (gout, gout_to))):
        copies.append(pltpu.make_async_copy(src, dst, sem.at[i]))
        copies[i].start()
    for copy in copies:
        copy.wait()


def shards(ny, nzl, frames, frame_keep, destination, ln_gain, ln_bias, w_in, w_out, upstream):
    nf, width = frames.shape
    nb = destination.shape[0]
    run = nf // nb
    rows = upstream.shape[0]
    cap = rows // (run * ny * 4)
    units = w_in.shape[1]
    half = units // NC
    own_rows = width // (ny * NZH)
    panels = half // LANE
    prow = panels * own_rows
    piece = -(-prow // (nzl * ROWS16)) * ROWS16
    per_core = nzl // NC
    nz = NZH * nzl
    ygroup = ny // NX
    nm = ygroup * 4
    mrows = -(-(width // LANE + 1) * cap * run // ROWS16) * ROWS16
    grad_scale = float(nf * ny * 4 * nzl) ** (-0.5)
    quarter = rows // NX
    ysteps, zsteps = ny // 2, nz // 2
    core_rows = own_rows // NC
    dma = pltpu.SemaphoreType.DMA
    vm = pltpu.VMEM
    pairs = [4, nm, 1, 16, 2 * OPARTS * ysteps, 2 * IPARTS * zsteps, nz - 1, ny - 1, (2, nzl), 1, NX - 1, NX - 1]
    sems = []
    for i, n in enumerate(pairs):
        shape = n if isinstance(n, tuple) else (n,)
        sems += [dma(shape)] if i == 0 else [dma(shape), dma(shape)]
    vspec = pl.BlockSpec(memory_space=pltpu.VMEM)
    aspec = pl.BlockSpec(memory_space=pl.ANY)
    enc, gin, gout = pl.pallas_call(
        functools.partial(kernel, (ny, nzl, cap, run, 0.5 * grad_scale)),
        out_shape=(
            jax.ShapeDtypeStruct((rows, width), BF16),
            jax.ShapeDtypeStruct((core_rows, units), F32),
            jax.ShapeDtypeStruct((core_rows, units), F32),
        ),
        in_specs=[vspec, vspec, aspec, vspec, vspec, aspec, aspec, aspec],
        out_specs=(vspec, vspec, vspec),
        scratch_shapes=[
            vm((width, half), BF16),
            vm((half, width), BF16),
            vm((nf, width), BF16),
            vm((rows, width), BF16),
            vm((nm * mrows, LANE), BF16),
            vm((nm * mrows, LANE), BF16),
            vm((NC * rows, width + LANE), BF16),
            vm((NC * rows, width), BF16),
            vm((width, NC * rows), BF16),
            vm((NC * rows, half), F32),
            vm((width, NC * rows), BF16),
            vm((NC * rows, half), BF16),
            vm((NC * rows, half), BF16),
            vm((NZH, ny, prow, LANE), BF16),
            vm((NZH, ny, prow, LANE), BF16),
            vm((2, OPARTS, ysteps, prow * NZH // OPARTS, LANE), BF16),
            vm((2, IPARTS, zsteps, ny // IPARTS, piece, LANE), BF16),
            vm((NZH, prow, LANE), BF16),
            vm((ny, piece, LANE), BF16),
            vm((nz - 1, piece, LANE), BF16),
            vm((ny - 1, piece, LANE), BF16),
            vm((2, piece, LANE), BF16),
            vm((2, NC * per_core, piece, LANE), BF16),
            vm((rows, width), F32),
            vm((rows, width), BF16),
            vm((rows, width), BF16),
            vm((rows, width), BF16),
            vm((NX - 1, quarter, width), BF16),
        ]
        + sems,
        compiler_params=pltpu.CompilerParams(
            collective_id=0, has_side_effects=True, vmem_limit_bytes=56 * 1024 * 1024
        ),
        name="ffn_step",
    )(
        destination.reshape(1, nb),
        frame_keep,
        frames,
        ln_gain.reshape(1, width),
        ln_bias.reshape(1, width),
        w_in,
        w_out,
        upstream,
    )
    enc, gin, gout = pl.pallas_call(
        place_outputs,
        out_shape=tuple(jax.ShapeDtypeStruct(v.shape, v.dtype) for v in (enc, gin, gout)),
        in_specs=[vspec] * 3,
        out_specs=(aspec,) * 3,
        scratch_shapes=[dma((3,))],
        name="place_outputs",
    )(enc, gin, gout)
    return (enc, gin, gout.T)


def solution(mesh):
    placed = (
        P(("dp", "mp"), None),
        P(("dp", "mp")),
        P(("dp", "mp"), None),
        P(),
        P(),
        P(None, "group"),
        P("group", None),
        P(("dp", "mp"), None),
    )
    ny = mesh.shape["dp"] // (NZH * NC)
    return jax.shard_map(
        functools.partial(shards, ny, mesh.shape["mp"]),
        mesh=mesh,
        in_specs=placed,
        out_specs=(P(("dp", "mp"), None), P("dp", "group"), P("group", "dp")),
        check_vma=False,
    )
```

```python
import functools
import jax
import jax.numpy as jnp
from jax import lax
from jax.experimental import pallas as pl
from jax.experimental.pallas import tpu as pltpu
from jax.sharding import PartitionSpec as P

MESH = pl.DeviceIdType.MESH
NX = 4
NC = 2
NZH = 2
LANE = 128
ROWS16 = 16
F32 = jnp.float32
BF16 = jnp.bfloat16
I32 = jnp.int32
OPARTS = 2
IPARTS = 2


def iota(shape, axis):
    return lax.broadcasted_iota(I32, shape, axis)


def dot(a, b):
    return jnp.dot(a, b, preferred_element_type=F32)


def kernel(
    dims,
    dest_ref,
    keep_ref,
    frames_hbm,
    gain_ref,
    bias_ref,
    w_in_hbm,
    w_out_hbm,
    up_hbm,
    enc_ref,
    gin_ref,
    gout_ref,
    w_in,
    w_out,
    frames_ref,
    up_ref,
    msg,
    arr,
    tok,
    ups,
    ups_t,
    back,
    nrm_t,
    hid,
    act,
    g_out,
    g_in,
    r_out,
    r_in,
    s_out,
    s_in,
    l_z,
    l_y,
    pce,
    fin,
    p_own,
    p_oth,
    p_rcv,
    q_sum,
    q_rcv,
    w_sem,
    a_snd,
    a_rcv,
    u_snd,
    u_rcv,
    t_snd,
    t_rcv,
    o_snd,
    o_rcv,
    i_snd,
    i_rcv,
    z_snd,
    z_rcv,
    y_snd,
    y_rcv,
    f_snd,
    f_rcv,
    p_snd,
    p_rsm,
    q_snd,
    q_rsm,
    e_snd,
    e_rcv,
):
    ny, nzl, cap, run, scale = dims
    nz = NZH * nzl
    rows, width = up_ref.shape
    half = w_in.shape[1]
    slab = rows // ny
    pair_rows = cap * run
    panels = half // LANE
    own_rows = width // (ny * NZH)
    prow = panels * own_rows
    core_rows = own_rows // NC
    core_span = panels * core_rows
    per_core = nzl // NC
    piece = pce.shape[1]
    quarter = rows // NX
    ygroup = ny // NX
    mrows = msg.shape[0] // (ygroup * 4)

    dp = lax.axis_index("dp")
    y = lax.div(dp, 4)
    zh = lax.rem(lax.div(dp, 2), 2)
    c = lax.rem(dp, 2)
    zl = lax.axis_index("mp")
    x = lax.axis_index("group")
    z = zh * nzl + zl
    pc = 1 - c

    def wrap(v, n):
        return lax.rem(v + n, n)

    def at_y(v):
        return {"dp": v * 4 + zh * 2 + c}

    def at_z(v):
        return {"dp": y * 4 + lax.div(v, nzl) * 2 + c, "mp": lax.rem(v, nzl)}

    def at_x(v):
        return {"group": v}

    partner = {"dp": y * 4 + zh * 2 + pc}

    started = []

    def flush(count):
        for copy in started[:count]:
            copy.wait_send()
        del started[:count]

    def send(src, dst, snd, rcv, where):
        copy = pltpu.make_async_remote_copy(
            src_ref=src, dst_ref=dst, send_sem=snd, recv_sem=rcv, device_id=where, device_id_type=MESH
        )
        copy.start()
        started.append(copy)
        return copy

    get_w_in = pltpu.make_async_copy(w_in_hbm.at[:, pl.ds(pl.multiple_of(c * half, half), half)], w_in, w_sem.at[0])
    get_w_out = pltpu.make_async_copy(w_out_hbm.at[pl.ds(pl.multiple_of(c * half, half), half), :], w_out, w_sem.at[1])

    get_frames = pltpu.make_async_copy(frames_hbm, frames_ref, w_sem.at[2])
    get_up = pltpu.make_async_copy(up_hbm, up_ref, w_sem.at[3])
    get_frames.start()

    barrier = pltpu.get_barrier_semaphore()
    greeted = 0
    kinds = [(g, dz, dc) for g in range(ygroup) for dz in range(2) for dc in range(2)]

    def a2a_id(yy, dz, dc):
        zz = (1 - zh) if dz else zh
        cc = pc if dc else c
        return {"dp": yy * 4 + zz * 2 + cc}

    sources = []
    for g, dz, dc in kinds:
        if dz or dc:
            sources.append(a2a_id(wrap(y - x - NX * g + ny, ny), dz, dc))
    sources += [at_y(wrap(y - d, ny)) for d in range(1, ny)]
    sources += [at_z(wrap(z - d, nz)) for d in range(1, nz)]
    sources += [at_x(wrap(x - d, NX)) for d in range(1, NX)]
    sources += [{"dp": y * 4 + zh * 2 + pc, "mp": wrap(zl - d, nzl)} for d in range(1, nzl)]
    sources += [partner]
    for where in sources:
        pl.semaphore_signal(barrier, inc=1, device_id=where, device_id_type=MESH)

    get_up.start()
    get_w_out.start()
    get_w_in.start()

    nb = dest_ref.shape[1]
    nf = nb * run
    bi, bj = iota((nb, nb), 0), iota((nb, nb), 1)
    drow = jnp.broadcast_to(dest_ref[...], (nb, nb))
    dcol = jnp.sum(jnp.where(bi == bj, drow, 0), axis=1, keepdims=True)
    rank = jnp.sum(jnp.where((dcol == drow) & (bi < bj), 1, 0), axis=0, keepdims=True)
    slot = (dest_ref[...] * cap + rank).astype(F32).astype(BF16)
    spread = (iota((nb, nf), 0) == lax.div(iota((nb, nf), 1), run)).astype(F32).astype(BF16)
    slot_f = dot(jnp.broadcast_to(slot, (8, nb)), spread)[0:1, :]
    nm = len(kinds)
    mi = iota((nm * ROWS16, 1), 0)
    mk, mr = lax.div(mi, ROWS16), lax.rem(mi, ROWS16)
    mg, mdz, mdc = lax.div(mk, 4), lax.rem(lax.div(mk, 2), 2), lax.rem(mk, 2)
    my = lax.rem(y + x + NX * mg, ny)
    mzh = lax.rem(zh + mdz, 2)
    mc = lax.rem(c + mdc, 2)
    want = ((my * 4 + mzh * 2 + mc) * cap + lax.div(mr, run)).astype(F32)
    shape = (nm * ROWS16, nf)
    hit = (
        (jnp.broadcast_to(slot_f, shape) == jnp.broadcast_to(want, shape))
        & (lax.rem(iota(shape, 1), run) == jnp.broadcast_to(lax.rem(mr, run), shape))
        & (jnp.broadcast_to(mr, shape) < pair_rows)
    )
    place = jnp.where(hit, 1.0, 0.0)
    keep_row = keep_ref[...].reshape(1, nf).astype(F32)
    keep_col = jnp.sum(place * keep_row, axis=1, keepdims=True)
    get_frames.wait()
    packed = dot(place.astype(BF16), frames_ref[...])
    flags = jnp.broadcast_to(keep_col, (nm * ROWS16, LANE))
    lanes = width // LANE
    spare = jnp.zeros((mrows - (lanes + 1) * pair_rows, LANE), F32)
    for k in range(nm):
        at = slice(k * ROWS16, k * ROWS16 + pair_rows)
        parts = [packed[at, j * LANE : (j + 1) * LANE] for j in range(lanes)] + [flags[at, :], spare]
        msg[pl.ds(k * mrows, mrows), :] = jnp.concatenate(parts, axis=0).astype(BF16)
    mine = pl.ds(pl.multiple_of(c * rows, rows), rows)
    theirs = pl.ds(pl.multiple_of(pc * rows, rows), rows)

    pl.semaphore_wait(barrier, len(sources))

    a2a = {}

    def a2a_send(k):
        g, dz, dc = kinds[k]
        spot = pl.ds(pl.multiple_of((g * 4 + zh * 2 + c) * mrows, ROWS16), mrows)
        part = msg.at[pl.ds(k * mrows, mrows), :]
        copy = pltpu.make_async_remote_copy(
            src_ref=part,
            dst_ref=arr.at[spot, :],
            send_sem=a_snd.at[k],
            recv_sem=a_rcv.at[k],
            device_id=a2a_id(lax.rem(y + x + NX * g, ny), dz, dc),
            device_id_type=MESH,
        )
        a2a[k] = copy
        if k:
            copy.start()
            return None
        local = pltpu.make_async_copy(part, arr.at[spot, :], a_rcv.at[k])

        @pl.when(x == 0)
        def _():
            local.start()

        @pl.when(x != 0)
        def _():
            copy.start()

        return local

    def back_of(where):
        u = ups[where, :]
        back[where, :] = lax.dot_general(u, w_out[...], (((1,), (1,)), ((), ())), preferred_element_type=F32)
        ups_t[:, where] = u.T

    locals_of = {}
    for k in (2, 3, 6, 7, 0, 1, 4, 5):
        locals_of[k] = a2a_send(k)
    local = locals_of[0]
    get_up.wait()
    ups[mine, :] = (scale * up_ref[...].astype(F32)).astype(BF16)
    ucopy = send(ups.at[mine, :], ups.at[mine, :], u_snd.at[0], u_rcv.at[0], partner)
    get_w_out.wait()
    back_of(mine)
    ucopy.wait_recv()
    back_of(theirs)
    get_w_in.wait()

    def rows_of(origin, g):
        ys = lax.rem(y - origin - NX * g + 2 * ny, ny)
        return tok.at[pl.ds(pl.multiple_of(c * rows + ys * slab, ROWS16), slab), :]

    def t_at(second, o, g):
        return second * 8 + o * 2 + g

    xn, xp, xo = wrap(x + 1, NX), wrap(x - 1, NX), wrap(x + 2, NX)
    origins = {0: x, 1: xn, 2: xo, 3: xp}

    def t_send(o, g, second, slot_at_receiver, tag, where):
        ref = rows_of(origins[o], g)
        return send(ref, ref, t_snd.at[tag], t_rcv.at[t_at(second, slot_at_receiver, g)], where)

    waits = {}
    for g in range(ygroup):
        for k in range(g * 4, g * 4 + 4):
            if k == 0:

                @pl.when(x == 0)
                def _():
                    local.wait()

                @pl.when(x != 0)
                def _():
                    a2a[0].wait()
            else:
                a2a[k].wait()
        got = arr[pl.ds(g * 4 * mrows, 4 * mrows), :].astype(F32)
        mine_now = rows_of(x, g)
        for j in range(lanes + 1):
            parts = [got[m * mrows + j * pair_rows : m * mrows + (j + 1) * pair_rows, :] for m in range(4)]
            mine_now[:, pl.ds(j * LANE, LANE)] = jnp.concatenate(parts, axis=0).astype(BF16)
        if g == 0:
            waits[3, g] = t_send(0, g, 0, 3, g, at_x(xn))
            waits[1, g] = t_send(0, g, 0, 1, 2 + g, at_x(xp))
        else:
            waits[1, g] = t_send(0, g, 0, 1, 2 + g, at_x(xp))
            waits[3, g] = t_send(0, g, 0, 3, g, at_x(xn))
        waits["c", 0, g] = t_send(0, g, 1, 0, 4 + g, partner)
    waits[3, 0].wait_recv()
    waits[2, 0] = t_send(3, 0, 0, 2, 6, at_x(xn))
    waits["c", 3, 0] = t_send(3, 0, 1, 3, 8, partner)
    waits[1, 1].wait_recv()
    waits[2, 1] = t_send(1, 1, 0, 2, 7, at_x(xp))
    waits["c", 1, 1] = t_send(1, 1, 1, 1, 9, partner)
    waits[1, 0].wait_recv()
    waits["c", 1, 0] = t_send(1, 0, 1, 1, 11, partner)
    waits[3, 1].wait_recv()
    waits["c", 3, 1] = t_send(3, 1, 1, 3, 10, partner)
    for g in range(ygroup):
        waits[2, g].wait_recv()
        waits["c", 2, g] = t_send(2, g, 1, 2, 12 + g, partner)
    step_rows = LANE

    def forward(begin):
        at = pl.ds(pl.multiple_of(begin, step_rows), step_rows)
        feat = tok[at, :width].astype(F32)
        live = tok[at, width:][:, 0:1].astype(F32)
        mean = jnp.mean(feat, axis=1, keepdims=True)
        cen = feat - mean
        var = jnp.mean(cen * cen, axis=1, keepdims=True)
        norm = (cen * lax.rsqrt(var + 1e-05) * gain_ref[...] + bias_ref[...]).astype(BF16)
        nrm_t[:, at] = norm.T
        pre = dot(norm, w_in[...])
        sig = jax.nn.sigmoid(pre)
        hid[at, :] = (live * (pre * sig)).astype(BF16)
        act[at, :] = (live * back[at, :] * (sig + pre * sig * (1.0 - sig))).astype(BF16)

    for t in range(rows // step_rows):
        forward(c * rows + t * step_rows)
    for o in (0, 3, 1, 2):
        for g in range(ygroup):
            waits["c", o, g].wait_recv()
    for t in range(rows // step_rows):
        forward(pc * rows + t * step_rows)

    def gradient(left, right, out):
        block = 2 * LANE
        for b in range(width // block):
            val = dot(left[pl.ds(b * block, block), :], right[...]).astype(BF16)
            for u in range(block // own_rows):
                unit = b * (block // own_rows) + u
                for e in range(NC):
                    for p in range(panels):
                        row = u * own_rows + e * core_rows
                        out[unit % NZH, unit // NZH, pl.ds((e * panels + p) * core_rows, core_rows), :] = val[
                            row : row + core_rows, p * LANE : (p + 1) * LANE
                        ]

    def start_of(j):
        core_at = lax.div(j, per_core)
        inside = jnp.minimum(lax.rem(j, per_core) * piece, core_span - piece)
        return pl.multiple_of(core_at * core_span + inside, ROWS16)

    ysteps = ny // 2
    ochain = {}
    ocut = OPARTS // NZH
    orows = prow // ocut

    def o_own(q, v):
        return g_out.at[q // ocut, v, pl.ds(q % ocut * orows, orows), :]

    def o_step(phase, s):
        for d in range(2):
            sign = 1 - 2 * d
            for q in range(OPARTS):
                if (d == q % 2) != (phase == 0):
                    continue
                first = 1 + phase
                own = o_own(q, wrap(y + sign * (ysteps + 1 - s), ny))
                if s == first:
                    src = own
                else:
                    ochain[d, q, s - 1].wait_recv()
                    src = r_out.at[d, q, s - 2]
                    src[...] = (src[...].astype(F32) + own[...].astype(F32)).astype(BF16)
                tag = (d * OPARTS + q) * ysteps + s - 1
                ochain[d, q, s] = send(
                    src, r_out.at[d, q, s - 1], o_snd.at[tag], o_rcv.at[tag], at_y(wrap(y + sign, ny))
                )

    zsteps = nz // 2
    ichain = {}
    hy = ny // IPARTS

    def i_own(q, v):
        return g_in.at[lax.div(v, nzl), pl.ds(q * hy, hy), pl.ds(start_of(lax.rem(v, nzl)), piece), :]

    def i_step(phase, s):
        for d in range(2):
            sign = 1 - 2 * d
            for q in range(IPARTS):
                if (d == q % 2) != (phase == 0):
                    continue
                first = 1 + phase
                own = i_own(q, wrap(z + sign * (zsteps + 1 - s), nz))
                if s == first:
                    src = own
                else:
                    ichain[d, q, s - 1].wait_recv()
                    src = r_in.at[d, q, s - 2]
                    src[...] = (src[...].astype(F32) + own[...].astype(F32)).astype(BF16)
                tag = (d * IPARTS + q) * zsteps + s - 1
                ichain[d, q, s] = send(
                    src, r_in.at[d, q, s - 1], i_snd.at[tag], i_rcv.at[tag], at_z(wrap(z + sign, nz))
                )

    gradient(nrm_t, act, g_in)
    i_step(0, 1)
    gradient(ups_t, hid, g_out)
    o_step(0, 1)
    i_step(1, 2)
    p_oth[...] = dot(hid[theirs, :], w_out[...]).astype(BF16)
    o_step(1, 2)
    pcopy = send(p_oth, p_rcv, p_snd.at[0], p_rsm.at[0], partner)
    i_step(0, 2)
    o_step(0, 2)
    p_own[...] = dot(hid[mine, :], w_out[...])
    i_step(1, 3)
    o_step(1, 3)
    i_step(0, 3)
    o_step(0, 3)
    pcopy.wait_recv()
    q_sum[...] = (p_own[...] + p_rcv[...].astype(F32)).astype(BF16)
    qcopies = []
    for d in range(1, NX):
        to = wrap(x + d, NX)
        part = q_sum.at[pl.ds(pl.multiple_of(to * quarter, quarter), quarter), :]
        qcopies.append(send(part, q_rcv.at[d - 1], q_snd.at[d - 1], q_rsm.at[d - 1], at_x(to)))
    i_step(1, 4)
    o_step(1, 4)
    i_step(0, 4)
    o_step(0, 4)
    i_step(1, 5)
    i_step(0, 5)

    zcopies = []
    for q in range(OPARTS):
        ochain[0, q, ysteps].wait_recv()
        ochain[1, q, ysteps].wait_recv()
        s_out[q // ocut, pl.ds(q % ocut * orows, orows), :] = (
            o_own(q, y)[...].astype(F32)
            + r_out[0, q, ysteps - 1].astype(F32)
            + r_out[1, q, ysteps - 1].astype(F32)
        ).astype(BF16)
    for d in range(1, nz):
        to = wrap(z + d, nz)
        part = s_out.at[lax.div(to, nzl), pl.ds(start_of(lax.rem(to, nzl)), piece), :]
        zcopies.append(send(part, l_z.at[d - 1], z_snd.at[d - 1], z_rcv.at[d - 1], at_z(to)))
    i_step(1, 6)
    i_step(0, 6)

    gone = len(started)
    for q in range(IPARTS):
        ichain[0, q, zsteps].wait_recv()
        ichain[1, q, zsteps].wait_recv()
        s_in[pl.ds(q * hy, hy)] = (
            i_own(q, z)[...].astype(F32)
            + r_in[0, q, zsteps - 1].astype(F32)
            + r_in[1, q, zsteps - 1].astype(F32)
        ).astype(BF16)
    ycopies = []
    for d in range(1, ny):
        to = wrap(y + d, ny)
        ycopies.append(send(s_in.at[to], l_y.at[d - 1], y_snd.at[d - 1], y_rcv.at[d - 1], at_y(to)))

    home = lax.div(zl, per_core)
    spot = c * per_core + lax.rem(zl, per_core)

    def gather(t):
        def base(d):
            return pltpu.make_async_remote_copy(
                src_ref=pce.at[t],
                dst_ref=fin.at[t, spot],
                send_sem=f_snd.at[t, d],
                recv_sem=f_rcv.at[t, spot],
                device_id={"dp": y * 4 + zh * 2 + home, "mp": wrap(zl + d, nzl)},
                device_id_type=MESH,
            )

        @pl.when(home == c)
        def _():
            pltpu.make_async_copy(pce.at[t], fin.at[t, spot], f_rcv.at[t, spot]).start()

        @pl.when(home != c)
        def _():
            base(0).start()

        for d in range(1, nzl):
            copy = base(d)
            copy.start()
            started.append(copy)
        return base(0)

    def gathered(t):
        for slot in range(NC * per_core):
            pltpu.make_async_copy(pce.at[t], fin.at[t, slot], f_rcv.at[t, slot]).wait()

    flush(gone)
    for q in zcopies:
        q.wait_recv()
    sum_out = s_out[zh, pl.ds(start_of(zl), piece), :].astype(F32)
    for d in range(1, nz):
        sum_out = sum_out + l_z[d - 1].astype(F32)
    pce[1] = sum_out.astype(BF16)
    own_out = gather(1)
    for q in qcopies:
        q.wait_recv()
    xrows = pl.ds(pl.multiple_of(x * quarter, quarter), quarter)
    total = q_sum[xrows, :].astype(F32)
    for d in range(1, NX):
        total = total + q_rcv[d - 1].astype(F32)
    trows = pl.ds(pl.multiple_of(c * rows + x * quarter, ROWS16), quarter)
    feat = tok[trows, :width].astype(F32)
    live = tok[trows, width:][:, 0:1].astype(F32)
    enc_ref[xrows, :] = (live * (feat + 0.5 * total)).astype(BF16)
    ecopies = []
    for d in range(1, NX):
        part = enc_ref.at[xrows, :]
        ecopies.append(send(part, part, e_snd.at[d - 1], e_rcv.at[d - 1], at_x(wrap(x + d, NX))))

    flush(len(started) - (nzl - 1))
    for q in ycopies:
        q.wait_recv()
    sum_in = s_in[y].astype(F32)
    for d in range(1, ny):
        sum_in = sum_in + l_y[d - 1].astype(F32)
    pce[0] = sum_in.astype(BF16)
    own_in = gather(0)
    gathered(1)
    gathered(0)

    @pl.when(home != c)
    def _():
        own_in.wait_send()
        own_out.wait_send()

    for e in range(NC):
        for u in range(core_span // ROWS16):
            row = u * ROWS16
            j = next(j for j in range(per_core) if row < min(j * piece, core_span - piece) + piece)
            off = row - min(j * piece, core_span - piece)
            p, r = row // core_rows, row % core_rows
            for t, ref in enumerate((gin_ref, gout_ref)):
                ref[pl.ds(r, ROWS16), pl.ds(e * half + p * LANE, LANE)] = fin[
                    t, e * per_core + j, pl.ds(off, ROWS16), :
                ].astype(F32)

    for q in ecopies:
        q.wait_recv()
    for q in started:
        q.wait_send()


def place_outputs(enc, gin, gout, enc_to, gin_to, gout_to, sem):
    copies = []
    for i, (src, dst) in enumerate(((enc, enc_to), (gin, gin_to), (gout, gout_to))):
        copies.append(pltpu.make_async_copy(src, dst, sem.at[i]))
        copies[i].start()
    for copy in copies:
        copy.wait()


def shards(ny, nzl, frames, frame_keep, destination, ln_gain, ln_bias, w_in, w_out, upstream):
    nf, width = frames.shape
    nb = destination.shape[0]
    run = nf // nb
    rows = upstream.shape[0]
    cap = rows // (run * ny * 4)
    units = w_in.shape[1]
    half = units // NC
    own_rows = width // (ny * NZH)
    panels = half // LANE
    prow = panels * own_rows
    piece = -(-prow // (nzl * ROWS16)) * ROWS16
    per_core = nzl // NC
    nz = NZH * nzl
    ygroup = ny // NX
    nm = ygroup * 4
    mrows = -(-(width // LANE + 1) * cap * run // ROWS16) * ROWS16
    grad_scale = float(nf * ny * 4 * nzl) ** (-0.5)
    quarter = rows // NX
    ysteps, zsteps = ny // 2, nz // 2
    core_rows = own_rows // NC
    dma = pltpu.SemaphoreType.DMA
    vm = pltpu.VMEM
    pairs = [4, nm, 1, 16, 2 * OPARTS * ysteps, 2 * IPARTS * zsteps, nz - 1, ny - 1, (2, nzl), 1, NX - 1, NX - 1]
    sems = []
    for i, n in enumerate(pairs):
        shape = n if isinstance(n, tuple) else (n,)
        sems += [dma(shape)] if i == 0 else [dma(shape), dma(shape)]
    vspec = pl.BlockSpec(memory_space=pltpu.VMEM)
    aspec = pl.BlockSpec(memory_space=pl.ANY)
    enc, gin, gout = pl.pallas_call(
        functools.partial(kernel, (ny, nzl, cap, run, 0.5 * grad_scale)),
        out_shape=(
            jax.ShapeDtypeStruct((rows, width), BF16),
            jax.ShapeDtypeStruct((core_rows, units), F32),
            jax.ShapeDtypeStruct((core_rows, units), F32),
        ),
        in_specs=[vspec, vspec, aspec, vspec, vspec, aspec, aspec, aspec],
        out_specs=(vspec, vspec, vspec),
        scratch_shapes=[
            vm((width, half), BF16),
            vm((half, width), BF16),
            vm((nf, width), BF16),
            vm((rows, width), BF16),
            vm((nm * mrows, LANE), BF16),
            vm((nm * mrows, LANE), BF16),
            vm((NC * rows, width + LANE), BF16),
            vm((NC * rows, width), BF16),
            vm((width, NC * rows), BF16),
            vm((NC * rows, half), F32),
            vm((width, NC * rows), BF16),
            vm((NC * rows, half), BF16),
            vm((NC * rows, half), BF16),
            vm((NZH, ny, prow, LANE), BF16),
            vm((NZH, ny, prow, LANE), BF16),
            vm((2, OPARTS, ysteps, prow * NZH // OPARTS, LANE), BF16),
            vm((2, IPARTS, zsteps, ny // IPARTS, piece, LANE), BF16),
            vm((NZH, prow, LANE), BF16),
            vm((ny, piece, LANE), BF16),
            vm((nz - 1, piece, LANE), BF16),
            vm((ny - 1, piece, LANE), BF16),
            vm((2, piece, LANE), BF16),
            vm((2, NC * per_core, piece, LANE), BF16),
            vm((rows, width), F32),
            vm((rows, width), BF16),
            vm((rows, width), BF16),
            vm((rows, width), BF16),
            vm((NX - 1, quarter, width), BF16),
        ]
        + sems,
        compiler_params=pltpu.CompilerParams(
            collective_id=0, has_side_effects=True, vmem_limit_bytes=56 * 1024 * 1024
        ),
        name="ffn_step",
    )(
        destination.reshape(1, nb),
        frame_keep,
        frames,
        ln_gain.reshape(1, width),
        ln_bias.reshape(1, width),
        w_in,
        w_out,
        upstream,
    )
    enc, gin, gout = pl.pallas_call(
        place_outputs,
        out_shape=tuple(jax.ShapeDtypeStruct(v.shape, v.dtype) for v in (enc, gin, gout)),
        in_specs=[vspec] * 3,
        out_specs=(aspec,) * 3,
        scratch_shapes=[dma((3,))],
        name="place_outputs",
    )(enc, gin, gout)
    return (enc, gin, gout.T)


def solution(mesh):
    placed = (
        P(("dp", "mp"), None),
        P(("dp", "mp")),
        P(("dp", "mp"), None),
        P(),
        P(),
        P(None, "group"),
        P("group", None),
        P(("dp", "mp"), None),
    )
    ny = mesh.shape["dp"] // (NZH * NC)
    return jax.shard_map(
        functools.partial(shards, ny, mesh.shape["mp"]),
        mesh=mesh,
        in_specs=placed,
        out_specs=(P(("dp", "mp"), None), P("dp", "group"), P("group", "dp")),
        check_vma=False,
    )
```
